32 devices in a mesh: seq: 8 (over y, x, core), mp: 4 (over z).
Axes of the slice: x: 2, y: 2, z: 4, core: 2. Of those that a mesh axis runs over, the one named last changes fastest.
Arguments:
- enc_states: bfloat16 [6144, 1280], P(('seq', 'mp')), may hold values from -6 to 6
- dec_states: bfloat16 [6144, 1280], P(('seq', 'mp')), may hold values from -240 to 240
- segments: int32 [6144], P(('seq', 'mp')), may hold values from 0 to 30, as said below
- patch_keys: bfloat16 [992, 1280], P(('seq', 'mp')), may hold values from -7 to 7
- w_in: bfloat16 [1280, 4096], P(None, 'mp'), may hold values from -0.15625 to 0.15625
- w_gate: bfloat16 [4096, 7168], P('seq', 'mp'), may hold values from -0.09375 to 0.09375
- w_up: bfloat16 [4096, 7168], P('seq', 'mp'), may hold values from -0.09375 to 0.09375
- w_down: bfloat16 [7168, 4096], P('mp', 'seq'), may hold values from -0.0625 to 0.0625
- w_out: bfloat16 [4096, 1280], P('mp'), may hold values from -0.09375 to 0.09375
Outputs:
- decoded: bfloat16 [6144, 1280], P(('seq', 'mp'))
The draws below stay inside these ranges and needn't reach their ends.
Inputs may be any that keep to these rules, and one draw needn't show every extreme that they name: `segments`: within each block of 192 bytes the patch number starts at 0 and rises by 0 or 1 from byte to byte. Block b belongs to device b, counted seq first; the blocks of the devices that share an mp index hold 128 patches together. A block holds at most 31 patches, and in every such set of blocks one holds exactly 31.
All inputs are finite; a program needn't handle non-finite values.
Results may differ from the reference program's by a relative error of at most 0.01.
Values may be sent and summed in bfloat16 or wider, within the bound.
No kernel may reach another device: no remote copies, remote signals or barrier semaphores. Data moves between devices by JAX's collectives and lax.ppermute only.
A program may use at most 128 MiB of HBM per device.

```python
import math
import jax
import jax.numpy as jnp
from jax import lax

E = 1280
HD = 128
D = 4096
FFW = 7168
BYTE_DEV = 192
RMEAN = 16
PMAX = 31
BYTES = 6144
PATCHES = 992
N_SEQ = 8
N_MP = 4


def counts_table(key):
    most_move = RMEAN // 3

    def column(column_key):
        shuffled = jax.random.permutation(jax.random.fold_in(column_key, 1), N_SEQ)
        shares = jax.random.randint(jax.random.fold_in(column_key, 2), (N_SEQ // 4,), 0, most_move + 1)
        shares = shares.at[0].set(most_move)
        ranking = jnp.zeros((N_SEQ,), jnp.int32).at[shuffled].set(jnp.arange(N_SEQ, dtype=jnp.int32))
        grouping = ranking // 4
        leader = ranking % 4 == 0
        amounts = shares[grouping]
        return jnp.where(leader, RMEAN + 3 * amounts, RMEAN - amounts).astype(jnp.int32)
    column_keys = jax.random.split(jax.random.fold_in(key, 11), N_MP)
    return jnp.transpose(jax.vmap(column)(column_keys))


def patch_numbers(key):
    totals = counts_table(key).reshape(N_SEQ * N_MP)

    def block(block_key, total):
        shuffled = jax.random.permutation(block_key, BYTE_DEV - 1)
        ranking = jnp.zeros((BYTE_DEV - 1,), jnp.int32).at[shuffled].set(jnp.arange(BYTE_DEV - 1, dtype=jnp.int32))
        is_cut = (ranking < total - 1).astype(jnp.int32)
        return jnp.concatenate([jnp.zeros((1,), jnp.int32), jnp.cumsum(is_cut).astype(jnp.int32)])
    block_keys = jax.random.split(jax.random.fold_in(key, 13), N_SEQ * N_MP)
    return jax.vmap(block)(block_keys, totals).reshape(BYTES)


def key_values(key):
    base = jnp.clip(jax.random.normal(jax.random.fold_in(key, 21), (PATCHES, E), jnp.float32), -6.0, 6.0)
    return base


def draw_segments(key, part):
    return patch_numbers(key)


def draw_patch_keys(key, part):
    return key_values(key).astype(jnp.bfloat16)


def draw_dec_states(key, part):
    base = jnp.clip(jax.random.normal(jax.random.fold_in(key, 31), (BYTES, E), jnp.float32), -6.0, 6.0)
    return base.astype(jnp.bfloat16)


def levels(key, dims, cuts, least, largest):
    def one(dim, blocks):
        draws = jax.random.uniform(jax.random.fold_in(jax.random.fold_in(key, 6), dim), (blocks,), jnp.float32, least / len(cuts), largest / len(cuts))
        return jnp.repeat(jnp.exp(draws), dims[dim] // blocks).reshape((-1,) + (1,) * (len(dims) - dim - 1))

    loudness = one(*cuts[0])
    for cut in cuts[1:]:
        loudness = loudness * one(*cut)
    return loudness


def bell_draw(rng, extent, spread, limit, pieces=(), kind=jnp.bfloat16):
    values = spread * jax.random.normal(rng, extent, jnp.float32)
    if pieces:
        values = values * levels(rng, extent, pieces, -0.22, 0.18)
    return jnp.clip(values, -limit, limit).astype(kind)


def setup_inputs(seed: int = 0) -> dict:
    key_of = jax.random.split(jax.random.key(seed), 10)
    enc_states = bell_draw(key_of[0], (BYTES, E), 1.0, 6.0, ((0, 32),))
    dec_states = draw_dec_states(jax.random.fold_in(key_of[9], 71), 0)
    segments = draw_segments(jax.random.fold_in(key_of[9], 71), 0)
    patch_keys = draw_patch_keys(jax.random.fold_in(key_of[9], 71), 0)
    w_in = bell_draw(key_of[4], (E, D), E ** -0.5, 0.15625, ((1, 4),))
    w_gate = bell_draw(key_of[5], (D, FFW), D ** -0.5, 0.09375, ((0, 8), (1, 4)))
    w_up = bell_draw(key_of[6], (D, FFW), D ** -0.5, 0.09375, ((0, 8), (1, 4)))
    w_down = bell_draw(key_of[7], (FFW, D), FFW ** -0.5, 0.0625, ((0, 4), (1, 8)))
    w_out = bell_draw(key_of[8], (D, E), D ** -0.5, 0.09375, ((0, 4),))
    return dict(enc_states=enc_states, dec_states=dec_states, segments=segments, patch_keys=patch_keys, w_in=w_in, w_gate=w_gate, w_up=w_up, w_down=w_down, w_out=w_out)


norm_epsilon = 1e-05

def reference(enc_states, dec_states, segments, patch_keys, w_in, w_gate, w_up, w_down, w_out):
    blocks = N_SEQ * N_MP
    heads = E // HD
    numbers = segments.reshape(blocks, BYTE_DEV)
    local_ids = jnp.arange(PMAX, dtype=jnp.int32)
    member = (numbers[:, None, :] == local_ids[None, :, None]).astype(jnp.float32)
    pool_sums = jnp.einsum('pjb,pbe->pje', member, enc_states.reshape(blocks, BYTE_DEV, E).astype(jnp.float32), precision=lax.Precision.HIGHEST)
    lengths = lax.optimization_barrier(jnp.sum(member, axis=2))
    pooled = (pool_sums / jnp.maximum(lengths, 1.0)[:, :, None]).astype(jnp.bfloat16)
    totals = numbers[:, BYTE_DEV - 1] + 1
    table = totals.reshape(N_SEQ, N_MP)
    starts = jnp.cumsum(table, axis=0).astype(jnp.int32) - table
    column_rows = N_SEQ * RMEAN
    all_rows = N_MP * column_rows
    first_row = (jnp.arange(N_MP, dtype=jnp.int32)[None, :] * column_rows + starts).reshape(blocks)
    index_rows = (first_row[:, None] + local_ids[None, :]).astype(jnp.int32)
    live = local_ids[None, :] < totals[:, None]
    target = jnp.where(live, index_rows, all_rows).astype(jnp.int32)
    packed = jnp.zeros((all_rows, E), jnp.bfloat16).at[target.reshape(-1)].set(pooled.reshape(blocks * PMAX, E), mode='drop')
    x_rows = jnp.dot(packed, w_in, preferred_element_type=jnp.float32).astype(jnp.bfloat16)
    x_wide = x_rows.astype(jnp.float32)
    square_mean = lax.optimization_barrier(jnp.mean(x_wide * x_wide, axis=1, keepdims=True))
    normed = (x_wide * lax.rsqrt(square_mean + norm_epsilon)).astype(jnp.bfloat16)
    gate = jnp.dot(normed, w_gate, preferred_element_type=jnp.float32)
    up = jnp.dot(normed, w_up, preferred_element_type=jnp.float32)
    hidden = (jax.nn.silu(gate) * up).astype(jnp.bfloat16)
    part_width = FFW // N_MP

    def add_part(total, index):
        piece_hidden = lax.dynamic_slice_in_dim(hidden, (index * part_width).astype(jnp.int32), part_width, 1)
        piece_weight = lax.dynamic_slice_in_dim(w_down, (index * part_width).astype(jnp.int32), part_width, 0)
        term = jnp.dot(piece_hidden, piece_weight, preferred_element_type=jnp.float32).astype(jnp.bfloat16)
        term = lax.optimization_barrier(term).astype(jnp.float32)
        return (total + term, None)
    down, _ = lax.scan(add_part, jnp.zeros((all_rows, D), jnp.float32), jnp.arange(N_MP, dtype=jnp.int32))
    residual = (x_wide + down).astype(jnp.bfloat16)
    model_part = D // N_MP

    def add_out(total, index):
        piece_rows = lax.dynamic_slice_in_dim(residual, (index * model_part).astype(jnp.int32), model_part, 1)
        piece_weight = lax.dynamic_slice_in_dim(w_out, (index * model_part).astype(jnp.int32), model_part, 0)
        term = jnp.dot(piece_rows, piece_weight, preferred_element_type=jnp.float32).astype(jnp.bfloat16)
        term = lax.optimization_barrier(term).astype(jnp.float32)
        return (total + term, None)
    out_sum, _ = lax.scan(add_out, jnp.zeros((all_rows, E), jnp.float32), jnp.arange(N_MP, dtype=jnp.int32))
    outputs = out_sum.astype(jnp.bfloat16)
    safe_rows = jnp.minimum(target, all_rows - 1).astype(jnp.int32)
    patch_values = jnp.take(outputs, safe_rows.reshape(-1), axis=0).reshape(blocks, PMAX, E)
    patch_values = jnp.where(live[:, :, None], patch_values, jnp.zeros_like(patch_values))
    queries = dec_states.reshape(blocks, BYTE_DEV, heads, HD).astype(jnp.float32)
    keys_local = patch_keys.reshape(blocks, PMAX, heads, HD).astype(jnp.float32)
    scores = jnp.einsum('pbhd,pjhd->phbj', queries, keys_local, precision=lax.Precision.HIGHEST) / math.sqrt(HD)
    allowed = local_ids[None, None, :] <= numbers[:, :, None]
    scores = jnp.where(allowed[:, None, :, :], scores, -1e+30)
    peak = lax.optimization_barrier(jnp.max(scores, axis=3, keepdims=True))
    expon = jnp.exp(scores - peak)
    weights = (expon / lax.optimization_barrier(jnp.sum(expon, axis=3, keepdims=True))).astype(jnp.bfloat16)
    values_local = patch_values.reshape(blocks, PMAX, heads, HD).astype(jnp.float32)
    mixed = jnp.einsum('phbj,pjhd->pbhd', weights.astype(jnp.float32), values_local, precision=lax.Precision.HIGHEST)
    return (dec_states.astype(jnp.float32) + mixed.reshape(BYTES, E)).astype(jnp.bfloat16)
```

```python
import functools
import math

import jax
import jax.numpy as jnp
from jax import lax
from jax.experimental import pallas as pl
from jax.experimental.pallas import tpu as pltpu
from jax.sharding import PartitionSpec as P

HD = 128
ROWS = 16
norm_epsilon = 1e-05

VMEM = pl.BlockSpec(memory_space=pltpu.VMEM)
SMEM = pl.BlockSpec(memory_space=pltpu.SMEM)
BF16 = jnp.bfloat16
F32 = jnp.float32


def shape(dims, dtype=BF16):
    return jax.ShapeDtypeStruct(tuple(dims), dtype)


def call(kernel, out, ids, *arrays, scratch=(), flops=0, limit=40):
    moved = sum(a.size * a.dtype.itemsize for a in arrays)
    moved += sum(math.prod(o.shape) * o.dtype.itemsize for o in jax.tree.leaves(out))
    return pl.pallas_call(
        kernel,
        out_shape=out,
        in_specs=[SMEM] + [VMEM] * len(arrays),
        out_specs=jax.tree.map(lambda _: VMEM, out),
        scratch_shapes=list(scratch),
        compiler_params=pltpu.CompilerParams(vmem_limit_bytes=limit * 1024 * 1024),
        cost_estimate=pl.CostEstimate(flops=int(flops), bytes_accessed=int(moved), transcendentals=0),
    )(ids, *arrays)


def dot(a, b):
    return jnp.dot(a, b, preferred_element_type=F32)


def pool_kernel(slots, ids, seg, enc, out):
    patch = lax.broadcasted_iota(jnp.int32, (slots, seg.shape[1]), 0)
    member = seg[...] == patch
    lengths = jnp.sum(member.astype(F32), axis=1, keepdims=True)
    sums = dot(member.astype(BF16), enc[...])
    pooled = sums / jnp.maximum(lengths, 1.0)
    total = jnp.max(seg[...].astype(F32)) + 1.0
    row = lax.broadcasted_iota(jnp.int32, pooled.shape, 0)
    out[...] = jnp.where(row == slots - 1, total, pooled).astype(BF16)


def pack_kernel(chips, slots, ids, *refs):
    mine, theirs = refs[:chips], refs[chips]
    out, start_out, packed = refs[chips + 1 :]
    q, c = ids[0], ids[1]
    blocks = 2 * chips
    lanes = blocks * slots
    for k in range(chips):
        packed[k * slots : (k + 1) * slots, :] = mine[k][...]
    packed[chips * slots :, :] = theirs[...]
    lane = lax.broadcasted_iota(jnp.int32, (1, lanes), 1)
    block = lane // slots
    patch = lane - block * slots
    part = block // chips
    place = 2 * ((block - part * chips) ^ q) + (part ^ c)
    start = jnp.zeros((1, lanes), F32)
    total = jnp.zeros((1, lanes), F32)
    own = jnp.zeros((1, lanes), F32)
    for b in range(blocks):
        count = packed[(b + 1) * slots - 1 : (b + 1) * slots, 0:lanes].astype(F32)
        where = 2 * ((b % chips) ^ q) + ((b // chips) ^ c)
        start += jnp.where(place > where, count, 0.0)
        total += jnp.where(block == b, count, 0.0)
        own += jnp.where(2 * q + c > where, count, 0.0)
    wanted = (2 * q + c) * ROWS + lax.broadcasted_iota(jnp.int32, (ROWS, lanes), 0)
    found = (start.astype(jnp.int32) + patch == wanted) & (patch < total.astype(jnp.int32))
    out[...] = dot(found.astype(BF16), packed[...]).astype(BF16)
    start_out[...] = jnp.broadcast_to(own[:, 0:HD].astype(jnp.int32), start_out.shape)


def x_kernel(groups, ids, *refs):
    pieces, w, out, packed = refs[:groups], refs[groups], refs[groups + 1], refs[groups + 2]
    for k in range(groups):
        packed[ids[2] ^ k] = pieces[k][...]
    rows = packed[...].reshape(groups * ROWS, packed.shape[2])
    out[...] = dot(rows, w[...]).astype(BF16)


def norm_kernel(groups, chips, ids, *refs):
    pieces, outs, units = refs[:groups], refs[groups : groups + chips], refs[groups + chips]
    q, c, z = ids[0], ids[1], ids[2]
    unit = units.shape[2]
    per = 2 * chips // groups
    squares = jnp.zeros((units.shape[1], 1), F32)
    for k in range(groups):
        wide = pieces[k][...].astype(F32)
        squares += jnp.sum(wide * wide, axis=1, keepdims=True)
        for u in range(per):
            units[(z ^ k) * per + u] = pieces[k][:, u * unit : (u + 1) * unit]
    scale = lax.rsqrt(squares / (2 * chips * unit) + norm_epsilon)
    for k in range(chips):
        for h in range(2):
            piece = units[2 * (q ^ k) + (c ^ h)].astype(F32)
            outs[k][h] = (piece * scale).astype(BF16)


def gate_kernel(count, ids, *refs):
    pieces = refs[:count]
    gate_a, gate_b, up_a, up_b = refs[count : count + 4]
    outs = refs[count + 4 :]
    rows, wide = pieces[0].shape[1], gate_a.shape[1]
    a = jnp.concatenate([p[0] for p in pieces], axis=0)
    b = jnp.concatenate([p[1] for p in pieces], axis=0)
    gate = (dot(a, gate_a[...]) + dot(b, gate_b[...])).astype(BF16)
    for k in range(count):
        outs[k][:, :wide] = gate[k * rows : (k + 1) * rows]
    up = (dot(a, up_a[...]) + dot(b, up_b[...])).astype(BF16)
    for k in range(count):
        outs[k][:, wide:] = up[k * rows : (k + 1) * rows]


def hidden_kernel(ids, *refs):
    pieces, out = refs[:-1], refs[-1]
    wide = out.shape[1]
    gate = sum(p[:, :wide].astype(F32) for p in pieces)
    up = sum(p[:, wide:].astype(F32) for p in pieces)
    out[...] = (gate / (1.0 + jnp.exp(-gate)) * up).astype(BF16)


def down_kernel(count, ids, *refs):
    pieces, w_a, w_b, outs = refs[:count], refs[count], refs[count + 1], refs[count + 2 :]
    rows = pieces[0].shape[0]
    a = jnp.concatenate([p[...] for p in pieces], axis=0)
    for h, w in enumerate((w_a, w_b)):
        y = dot(a, w[...]).astype(BF16)
        for k in range(count):
            outs[k][h] = y[k * rows : (k + 1) * rows]


def regroup_kernel(chips, groups, ids, *refs):
    pieces, outs, units = refs[:chips], refs[chips : chips + groups], refs[chips + groups]
    q, c, z = ids[0], ids[1], ids[2]
    unit = units.shape[2]
    per = 2 * chips // groups
    for k in range(chips):
        for h in range(2):
            units[2 * (q ^ k) + (c ^ h)] = pieces[k][h]
    for k in range(groups):
        for u in range(per):
            outs[k][:, u * unit : (u + 1) * unit] = units[(z ^ k) * per + u]


def out_kernel(groups, ids, *refs):
    pieces, x, w, outs, rows = refs[:groups], refs[groups], refs[groups + 1], refs[groups + 2 : -1], refs[-1]
    down = sum(p[...].astype(F32) for p in pieces)
    residual = (x[...].astype(F32) + down).astype(BF16)
    y = dot(residual, w[...]).astype(BF16)
    rows[...] = y.reshape(rows.shape)
    for k in range(groups):
        outs[k][...] = rows[ids[2] ^ k]


def add_kernel(ids, *refs):
    refs[-1][...] = sum(p[...].astype(F32) for p in refs[:-1]).astype(BF16)


def weights_kernel(ids, seg, dec, keys, out):
    slots = keys.shape[0]
    patch = lax.broadcasted_iota(jnp.int32, (dec.shape[0], slots), 1)
    allowed = patch <= seg[...]
    for h in range(out.shape[0]):
        part = slice(h * HD, (h + 1) * HD)
        scores = lax.dot_general(dec[:, part], keys[:, part], (((1,), (1,)), ((), ())), preferred_element_type=F32)
        scores = jnp.where(allowed, scores / math.sqrt(HD), -1e30)
        expon = jnp.exp(scores - jnp.max(scores, axis=1, keepdims=True))
        out[h] = (expon / jnp.sum(expon, axis=1, keepdims=True)).astype(BF16)


def mix_kernel(chips, ids, *refs):
    mine, theirs = refs[:chips], refs[chips]
    start, weights, dec, out, rows = refs[chips + 1 :]
    q, c = ids[0], ids[1]
    for k in range(chips):
        rows[2 * (q ^ k) + c] = mine[k][...]
        rows[2 * (q ^ k) + 1 - c] = theirs[k]
    every = rows[...].reshape(2 * chips * ROWS, rows.shape[2])
    slots = weights.shape[2]
    patch = lax.broadcasted_iota(jnp.int32, (slots, every.shape[0]), 0)
    position = lax.broadcasted_iota(jnp.int32, (slots, every.shape[0]), 1)
    found = (position - start[0:1, 0:1] == patch).astype(BF16)
    values = dot(found, every).astype(BF16)
    for h in range(weights.shape[0]):
        part = slice(h * HD, (h + 1) * HD)
        out[:, part] = (dec[:, part].astype(F32) + dot(weights[h], values[:, part])).astype(BF16)


def body(enc_states, dec_states, segments, patch_keys, w_in, w_gate, w_up, w_down, w_out):
    seq, groups = lax.axis_size("seq"), lax.axis_size("mp")
    chips = seq // 2
    bytes_, width = enc_states.shape
    slots = patch_keys.shape[0] + 1
    heads = width // HD
    rows = groups * ROWS
    wide = w_in.shape[1]
    unit = w_gate.shape[0]
    ffw = w_gate.shape[1]
    index = lax.axis_index("seq")
    ids = jnp.stack([index // 2, index % 2, lax.axis_index("mp")]).astype(jnp.int32)

    def sibling(a):
        return lax.ppermute(a, "seq", [(i, i ^ 1) for i in range(seq)])

    def chip(a, k):
        return lax.ppermute(a, "seq", [(i, i ^ (2 * k)) for i in range(seq)])

    def plane(a, k):
        return lax.ppermute(a, "mp", [(i, i ^ k) for i in range(groups)])

    pooled = call(functools.partial(pool_kernel, slots), shape((slots, width)), ids, segments.reshape(1, bytes_), enc_states)
    gathered = [pooled] + [chip(pooled, k) for k in range(1, chips)]
    theirs = sibling(jnp.concatenate(gathered, axis=0))
    packed, start = call(
        functools.partial(pack_kernel, chips, slots),
        (shape((ROWS, width)), shape((8, HD), jnp.int32)),
        ids,
        *gathered,
        theirs,
        scratch=[pltpu.VMEM((seq * slots, width), BF16)],
    )
    gate_b, up_b, down_b = sibling(w_gate), sibling(w_up), sibling(w_down)
    pieces = [packed] + [plane(packed, k) for k in range(1, groups)]
    x = call(
        functools.partial(x_kernel, groups),
        shape((rows, wide)),
        ids,
        *pieces,
        w_in,
        scratch=[pltpu.VMEM((groups, ROWS, width), BF16)],
        flops=2 * rows * width * wide,
    )
    pieces = [x] + [plane(x, k) for k in range(1, groups)]
    normed = call(
        functools.partial(norm_kernel, groups, chips),
        [shape((2, rows, unit)) for _ in range(chips)],
        ids,
        *pieces,
        scratch=[pltpu.VMEM((seq, rows, unit), BF16)],
    )

    def gate(pieces):
        return call(
            functools.partial(gate_kernel, len(pieces)),
            [shape((rows, 2 * ffw)) for _ in pieces],
            ids,
            *pieces,
            w_gate,
            gate_b,
            w_up,
            up_b,
            flops=8 * len(pieces) * rows * unit * ffw,
        )

    arrived = [chip(normed[k], k) for k in range(1, chips)]
    partial = gate([normed[0]]) + gate(arrived)
    partial = [partial[0]] + [chip(partial[k], k) for k in range(1, chips)]
    hidden = call(hidden_kernel, shape((rows, ffw)), ids, *partial)

    def down(pieces):
        return call(
            functools.partial(down_kernel, len(pieces)),
            [shape((2, rows, unit)) for _ in pieces],
            ids,
            *pieces,
            w_down,
            down_b,
            flops=4 * len(pieces) * rows * unit * ffw,
        )

    arrived = [chip(hidden, k) for k in range(1, chips)]
    columns = down([hidden]) + down(arrived)
    columns = [columns[0]] + [chip(columns[k], k) for k in range(1, chips)]
    slices = call(
        functools.partial(regroup_kernel, chips, groups),
        [shape((rows, wide)) for _ in range(groups)],
        ids,
        *columns,
        scratch=[pltpu.VMEM((seq, rows, unit), BF16)],
    )
    slices = [slices[0]] + [plane(slices[k], k) for k in range(1, groups)]
    outs = call(
        functools.partial(out_kernel, groups),
        [shape((ROWS, width)) for _ in range(groups)],
        ids,
        *slices,
        x,
        w_out,
        scratch=[pltpu.VMEM((groups, ROWS, width), BF16)],
        flops=2 * rows * width * wide,
    )
    outs = [outs[0]] + [plane(outs[k], k) for k in range(1, groups)]
    outputs = call(add_kernel, shape((ROWS, width)), ids, *outs)
    outputs = [outputs] + [chip(outputs, k) for k in range(1, chips)]
    theirs = sibling(jnp.stack(outputs))
    keys = jnp.pad(patch_keys, ((0, 1), (0, 0)))
    weights = call(weights_kernel, shape((heads, bytes_, slots)), ids, segments.reshape(bytes_, 1), dec_states, keys)
    return call(
        functools.partial(mix_kernel, chips),
        shape((bytes_, width)),
        ids,
        *outputs,
        theirs,
        start,
        weights,
        dec_states,
        scratch=[pltpu.VMEM((seq, ROWS, width), BF16)],
    )


def solution(mesh):
    placed = (
        P(("seq", "mp"), None),
        P(("seq", "mp"), None),
        P(("seq", "mp")),
        P(("seq", "mp"), None),
        P(None, "mp"),
        P("seq", "mp"),
        P("seq", "mp"),
        P("mp", "seq"),
        P("mp", None),
    )
    return jax.shard_map(
        body, mesh=mesh, in_specs=placed, out_specs=P(("seq", "mp"), None), check_vma=False
    )
```

```python
import functools
import math

import jax
import jax.numpy as jnp
from jax import lax
from jax.experimental import pallas as pl
from jax.experimental.pallas import tpu as pltpu
from jax.sharding import PartitionSpec as P

HD = 128
ROWS = 16
norm_epsilon = 1e-05

VMEM = pl.BlockSpec(memory_space=pltpu.VMEM)
SMEM = pl.BlockSpec(memory_space=pltpu.SMEM)
HBM = pl.BlockSpec(memory_space=pl.ANY)
BF16 = jnp.bfloat16
F32 = jnp.float32


def shape(dims, dtype=BF16):
    return jax.ShapeDtypeStruct(tuple(dims), dtype)


def call(kernel, outs, ids, *arrays, hbm=(), through=(), scratch=(), flops=0, limit=40):
    n, t, o = len(arrays), len(through), len(outs)

    def run(ids, *refs):
        kernel(ids, *refs[:n], *refs[n + t : n + t + o], *refs[n + 2 * t + o :])

    moved = sum(a.size * a.dtype.itemsize for a in arrays)
    moved += sum(math.prod(a.shape) * a.dtype.itemsize for a in outs)
    return pl.pallas_call(
        run,
        out_shape=list(outs) + [shape(a.shape, a.dtype) for a in through],
        in_specs=[SMEM] + [HBM if i in hbm else VMEM for i in range(n)] + [HBM] * t,
        out_specs=[VMEM] * o + [HBM] * t,
        scratch_shapes=list(scratch),
        input_output_aliases={1 + n + i: o + i for i in range(t)},
        compiler_params=pltpu.CompilerParams(vmem_limit_bytes=limit * 1024 * 1024),
        cost_estimate=pl.CostEstimate(flops=int(flops), bytes_accessed=int(moved), transcendentals=0),
    )(ids, *arrays, *through)


def dot(a, b):
    return jnp.dot(a, b, preferred_element_type=F32)


def pool_kernel(slots, ids, seg_in, enc_in, out, seg, enc, sems):
    copies = [
        pltpu.make_async_copy(seg_in, seg, sems.at[0]),
        pltpu.make_async_copy(enc_in, enc, sems.at[1]),
    ]
    for copy in copies:
        copy.start()
    for copy in copies:
        copy.wait()
    patch = lax.broadcasted_iota(jnp.int32, (slots, seg.shape[1]), 0)
    member = seg[...] == patch
    lengths = jnp.sum(member.astype(F32), axis=1, keepdims=True)
    sums = dot(member.astype(BF16), enc[...])
    pooled = sums / jnp.maximum(lengths, 1.0)
    total = jnp.max(seg[...].astype(F32)) + 1.0
    row = lax.broadcasted_iota(jnp.int32, pooled.shape, 0)
    out[...] = jnp.where(row == slots - 1, total, pooled).astype(BF16)


def pack_kernel(chips, slots, ids, *refs):
    mine, theirs = refs[:chips], refs[chips]
    out, start_out, select_out, packed = refs[chips + 1 :]
    q, c = ids[0], ids[1]
    blocks = 2 * chips
    lanes = blocks * slots
    for k in range(chips):
        packed[k * slots : (k + 1) * slots, :] = mine[k][...]
    packed[chips * slots :, :] = theirs[...]
    lane = lax.broadcasted_iota(jnp.int32, (1, lanes), 1)
    block = lane // slots
    patch = lane - block * slots
    part = block // chips
    place = 2 * ((block - part * chips) ^ q) + (part ^ c)
    line, column = (lax.broadcasted_iota(jnp.int32, select_out.shape, d) for d in range(2))
    target = 2 * ((line // (2 * ROWS)) ^ q) + (((line // ROWS) % 2) ^ c)
    start = jnp.zeros((1, lanes), F32)
    total = jnp.zeros((1, lanes), F32)
    own = jnp.zeros((1, lanes), F32)
    target_start = jnp.zeros(select_out.shape, F32)
    target_total = jnp.zeros(select_out.shape, F32)
    for b in range(blocks):
        count = packed[(b + 1) * slots - 1 : (b + 1) * slots, 0:lanes].astype(F32)
        where = 2 * ((b % chips) ^ q) + ((b // chips) ^ c)
        start += jnp.where(place > where, count, 0.0)
        total += jnp.where(block == b, count, 0.0)
        own += jnp.where(2 * q + c > where, count, 0.0)
        count = count[:, : select_out.shape[1]]
        target_start += jnp.where(target > where, count, 0.0)
        target_total += jnp.where(target == where, count, 0.0)
    wanted = 2 * (q * ROWS + lax.broadcasted_iota(jnp.int32, (ROWS, lanes), 0)) + c
    found = (start.astype(jnp.int32) + patch == wanted) & (patch < total.astype(jnp.int32))
    out[...] = dot(found.astype(BF16), packed[...]).astype(BF16)
    start_out[...] = jnp.broadcast_to(own[:, 0:HD].astype(jnp.int32), start_out.shape)
    first = target_start.astype(jnp.int32)
    patch = ((c - first) & 1) + 2 * (line % ROWS)
    position = 2 * (((column // ROWS) ^ q) * ROWS + column % ROWS) + c
    found = (first + patch == position) & (patch < target_total.astype(jnp.int32))
    select_out[...] = found.astype(BF16)


def x_kernel(groups, ids, *refs):
    pieces, w_in = refs[:groups], refs[groups]
    out, packed, w, sems = refs[groups + 1 :]
    wide = w.shape[1]
    step = 256 if wide % 256 == 0 else wide
    copies = []
    for i in range(wide // step):
        part = pl.ds(i * step, step)
        copies.append(pltpu.make_async_copy(w_in.at[:, part], w.at[:, part], sems.at[i]))
        copies[-1].start()
    for k in range(groups):
        packed[ids[2] ^ k] = pieces[k][...]
    rows = packed[...].reshape(groups * ROWS, packed.shape[2])
    for i, copy in enumerate(copies):
        copy.wait()
        part = slice(i * step, (i + 1) * step)
        out[:, part] = dot(rows, w[:, part]).astype(BF16)


def spread_kernel(groups, chips, ids, *refs):
    pieces, outs, scale, units = refs[:groups], refs[groups : groups + chips], refs[-2], refs[-1]
    q, c, z = ids[0], ids[1], ids[2]
    unit = units.shape[2]
    per = 2 * chips // groups
    for k in range(groups):
        for u in range(per):
            units[(z ^ k) * per + u] = pieces[k][:, u * unit : (u + 1) * unit]
    for k in range(chips):
        for h in range(2):
            outs[k][h] = units[2 * (q ^ k) + (c ^ h)]
    squares = jnp.zeros((units.shape[1], 1), F32)
    for k in range(groups):
        wide = pieces[k][...].astype(F32)
        squares += jnp.sum(wide * wide, axis=1, keepdims=True)
    scale[...] = jnp.broadcast_to(lax.rsqrt(squares / (2 * chips * unit) + norm_epsilon), scale.shape)


def gate_kernel(ids, piece, gate_a, gate_b, up_a, up_b, out):
    wide = gate_a.shape[1]
    a, b = piece[0], piece[1]
    out[:, :wide] = (dot(a, gate_a[...]) + dot(b, gate_b[...])).astype(BF16)
    out[:, wide:] = (dot(a, up_a[...]) + dot(b, up_b[...])).astype(BF16)


def hidden_kernel(ids, scale, *refs):
    pieces, out = refs[:-1], refs[-1]
    wide = out.shape[1]
    gate = sum(p[:, :wide].astype(F32) for p in pieces) * scale[:, 0:1]
    up = sum(p[:, wide:].astype(F32) for p in pieces) * scale[:, 0:1]
    out[...] = (gate / (1.0 + jnp.exp(-gate)) * up).astype(BF16)


def down_kernel(chips, groups, ids, *refs):
    pieces, ws, outs, held = refs[:chips], refs[chips : chips + 2], refs[chips + 2 : -1], refs[-1]
    rows = jnp.concatenate([p[...] for p in pieces], axis=0)
    unit = ws[0].shape[1]
    for h, w in enumerate(ws):
        y = dot(rows, w[...]).astype(BF16)
        held[:, :, :, h * unit : (h + 1) * unit] = y.reshape(chips, groups, ROWS, unit)
    for m in range(groups):
        for k in range(chips):
            outs[m][k * ROWS : (k + 1) * ROWS, :] = held[k, ids[2] ^ m]


def out_kernel(chips, groups, ids, *refs):
    sums, refs = refs[:groups], refs[groups:]
    xs, refs = refs[:chips], refs[chips:]
    ws, select, outs = refs[:4], refs[4], refs[5:]
    unit = xs[0].shape[2]
    mine = pl.ds(pl.multiple_of(ids[2] * ROWS, ROWS), ROWS)
    y = None
    for h in range(2):
        part = slice(h * unit, (h + 1) * unit)
        x = jnp.concatenate([p[h, mine, :] for p in xs], axis=0)
        down = sum(p[:, part].astype(F32) for p in sums)
        residual = (x.astype(F32) + down).astype(BF16)
        for i in range(2):
            w = ws[2 * h + i]
            term = dot(residual[:, i * w.shape[0] : (i + 1) * w.shape[0]], w[...])
            y = term if y is None else y + term
    rows = dot(select[...], y.astype(BF16)).astype(BF16)
    for k in range(chips):
        outs[k][...] = rows[k * 2 * ROWS : (k + 1) * 2 * ROWS]


def add_kernel(ids, *refs):
    pieces, mine, theirs = refs[:-2], refs[-2], refs[-1]
    total = sum(p[...].astype(F32) for p in pieces).astype(BF16)
    mine[...] = total[:ROWS]
    theirs[...] = total[ROWS:]


def pick_kernel(groups, ids, *refs):
    sources, out, sem = refs[:groups], refs[groups], refs[groups + 1]
    for h in range(groups):

        @pl.when((ids[0] ^ ids[2]) == h)
        def _():
            copy = pltpu.make_async_copy(sources[h], out, sem)
            copy.start()
            copy.wait()


def weights_kernel(ids, seg, dec, keys, out):
    slots = keys.shape[0]
    patch = lax.broadcasted_iota(jnp.int32, (dec.shape[0], slots), 1)
    allowed = patch <= seg[...]
    for h in range(out.shape[0]):
        part = slice(h * HD, (h + 1) * HD)
        scores = lax.dot_general(dec[:, part], keys[:, part], (((1,), (1,)), ((), ())), preferred_element_type=F32)
        scores = jnp.where(allowed, scores / math.sqrt(HD), -1e30)
        expon = jnp.exp(scores - jnp.max(scores, axis=1, keepdims=True))
        out[h] = (expon / jnp.sum(expon, axis=1, keepdims=True)).astype(BF16)


def mix_kernel(ids, mine, theirs, start, weights, dec, out):
    c = ids[1]
    slots = weights.shape[2]
    every = jnp.concatenate([mine[...], theirs[...]], axis=0)
    patch = lax.broadcasted_iota(jnp.int32, (slots, 2 * ROWS), 0)
    line = lax.broadcasted_iota(jnp.int32, (slots, 2 * ROWS), 1)
    parity = (c + line // ROWS - start[0:1, 0:1]) & 1
    values = dot((patch == parity + 2 * (line % ROWS)).astype(BF16), every).astype(BF16)
    for h in range(weights.shape[0]):
        part = slice(h * HD, (h + 1) * HD)
        out[:, part] = (dec[:, part].astype(F32) + dot(weights[h], values[:, part])).astype(BF16)


def body(enc_states, dec_states, segments, patch_keys, w_in, w_gate, w_up, w_down, w_out):
    seq, groups = lax.axis_size("seq"), lax.axis_size("mp")
    chips = seq // 2
    bytes_, width = enc_states.shape
    slots = patch_keys.shape[0] + 1
    heads = width // HD
    rows = groups * ROWS
    wide = w_in.shape[1]
    unit = w_gate.shape[0]
    ffw = w_gate.shape[1]
    index = lax.axis_index("seq")
    ids = jnp.stack([index // 2, index % 2, lax.axis_index("mp")]).astype(jnp.int32)

    def sibling(a):
        return lax.ppermute(a, "seq", [(i, i ^ 1) for i in range(seq)])

    def chip(a, k):
        return lax.ppermute(a, "seq", [(i, i ^ (2 * k)) for i in range(seq)])

    def plane(a, k):
        return lax.ppermute(a, "mp", [(i, i ^ k) for i in range(groups)])

    def spread_along(a, h, o):
        pairs = [(s * groups + ((s // 2) ^ h), s * groups + ((s // 2) ^ h ^ o)) for s in range(seq)]
        return lax.ppermute(a, ("seq", "mp"), pairs)

    def tree(a, have, offsets):
        have = dict(have)
        for o in offsets:
            for h in list(have):
                have[h ^ o] = spread_along(have[h], h, o)
        return have

    offsets = [1 << i for i in reversed(range(groups.bit_length() - 1))]
    half = unit // 2
    out_a = lax.dynamic_slice_in_dim(w_out, ids[1] * unit, half, 0)
    out_b = lax.dynamic_slice_in_dim(w_out, ids[1] * unit + half, half, 0)
    far_a = spread_along(out_a, 0, offsets[0])

    [pooled] = call(
        functools.partial(pool_kernel, slots),
        [shape((slots, width))],
        ids,
        segments.reshape(1, bytes_),
        enc_states,
        hbm=(0, 1),
        scratch=[
            pltpu.VMEM((1, bytes_), jnp.int32),
            pltpu.VMEM((bytes_, width), BF16),
            pltpu.SemaphoreType.DMA((2,)),
        ],
    )
    gathered = [pooled] + [chip(pooled, k) for k in range(1, chips)]
    theirs = sibling(jnp.concatenate(gathered, axis=0))
    packed, start, select = call(
        functools.partial(pack_kernel, chips, slots),
        [shape((ROWS, width)), shape((8, HD), jnp.int32), shape((seq * ROWS, chips * ROWS))],
        ids,
        *gathered,
        theirs,
        scratch=[pltpu.VMEM((seq * slots, width), BF16)],
    )
    gate_b, up_b, down_b = sibling(w_gate), sibling(w_up), sibling(w_down)
    pieces = [packed] + [plane(packed, k) for k in range(1, groups)]
    [x] = call(
        functools.partial(x_kernel, groups),
        [shape((rows, wide))],
        ids,
        *pieces,
        w_in,
        hbm=(groups,),
        scratch=[
            pltpu.VMEM((groups, ROWS, width), BF16),
            pltpu.VMEM((width, wide), BF16),
            pltpu.SemaphoreType.DMA((max(1, wide // 256),)),
        ],
        flops=2 * rows * width * wide,
    )
    pieces = [x] + [plane(x, k) for k in range(1, groups)]
    *xs, scale, out_a, out_b, far_a = call(
        functools.partial(spread_kernel, groups, chips),
        [shape((2, rows, unit)) for _ in range(chips)] + [shape((rows, HD), F32)],
        ids,
        *pieces,
        through=[out_a, out_b, far_a],
        scratch=[pltpu.VMEM((seq, rows, unit), BF16)],
    )

    def gate(piece, through=()):
        return call(
            gate_kernel,
            [shape((rows, 2 * ffw))],
            ids,
            piece,
            w_gate,
            gate_b,
            w_up,
            up_b,
            through=through,
            flops=8 * rows * unit * ffw,
        )

    far_b = spread_along(out_b, 0, offsets[0])
    partial, out_a, out_b, far_a = gate(xs[0], [out_a, out_b, far_a])
    xs = [xs[0]] + [chip(xs[k], k) for k in range(1, chips)]
    partial = [partial] + [chip(gate(xs[k])[0], k) for k in range(1, chips)]
    all_a = tree(out_a, {0: out_a, offsets[0]: far_a}, offsets[1:])
    all_b = tree(out_b, {0: out_b, offsets[0]: far_b}, offsets[1:])

    keys = jnp.pad(patch_keys, ((0, 1), (0, 0)))
    [weights] = call(
        weights_kernel, [shape((heads, bytes_, slots))], ids, segments.reshape(bytes_, 1), dec_states, keys
    )
    hidden, weights = call(hidden_kernel, [shape((rows, ffw))], ids, scale, *partial, through=[weights])
    hidden = [hidden] + [chip(hidden, k) for k in range(1, chips)]
    sums = call(
        functools.partial(down_kernel, chips, groups),
        [shape((chips * ROWS, 2 * unit)) for _ in range(groups)],
        ids,
        *hidden,
        w_down,
        down_b,
        scratch=[pltpu.VMEM((chips, groups, ROWS, 2 * unit), BF16)],
        flops=4 * chips * rows * unit * ffw,
    )
    sums = [sums[0]] + [plane(sums[k], k) for k in range(1, groups)]

    def pick(have):
        [mine] = call(
            functools.partial(pick_kernel, groups),
            [shape((half, width))],
            ids,
            *[have[h] for h in range(groups)],
            hbm=range(groups),
            scratch=[pltpu.SemaphoreType.DMA],
        )
        return mine

    mine_a, mine_b = pick(all_a), pick(all_b)
    outs = call(
        functools.partial(out_kernel, chips, groups),
        [shape((2 * ROWS, width)) for _ in range(chips)],
        ids,
        *sums,
        *xs,
        mine_a,
        mine_b,
        sibling(mine_a),
        sibling(mine_b),
        select,
        flops=2 * rows * width * wide,
    )
    outs = [outs[0]] + [chip(outs[k], k) for k in range(1, chips)]
    mine, theirs = call(add_kernel, [shape((ROWS, width))] * 2, ids, *outs)
    [decoded] = call(
        mix_kernel, [shape((bytes_, width))], ids, mine, sibling(theirs), start, weights, dec_states
    )
    return decoded


def solution(mesh):
    placed = (
        P(("seq", "mp"), None),
        P(("seq", "mp"), None),
        P(("seq", "mp")),
        P(("seq", "mp"), None),
        P(None, "mp"),
        P("seq", "mp"),
        P("seq", "mp"),
        P("mp", "seq"),
        P("mp", None),
    )
    return jax.shard_map(
        body, mesh=mesh, in_specs=placed, out_specs=P(("seq", "mp"), None), check_vma=False
    )
```

```python
import functools
import math

import jax
import jax.numpy as jnp
from jax import lax
from jax.experimental import pallas as pl
from jax.experimental.pallas import tpu as pltpu
from jax.sharding import PartitionSpec as P

HD = 128
ROWS = 16
norm_epsilon = 1e-05

VMEM = pl.BlockSpec(memory_space=pltpu.VMEM)
SMEM = pl.BlockSpec(memory_space=pltpu.SMEM)
HBM = pl.BlockSpec(memory_space=pl.ANY)
BF16 = jnp.bfloat16
F32 = jnp.float32


def shape(dims, dtype=BF16):
    return jax.ShapeDtypeStruct(tuple(dims), dtype)


def call(kernel, outs, ids, *arrays, hbm=(), through=(), scratch=(), flops=0, limit=20):
    n, t, o = len(arrays), len(through), len(outs)

    def run(ids, *refs):
        kernel(ids, *refs[:n], *refs[n + t : n + t + o], *refs[n + 2 * t + o :])

    moved = sum(a.size * a.dtype.itemsize for a in arrays)
    moved += sum(math.prod(a.shape) * a.dtype.itemsize for a in outs)
    results = pl.pallas_call(
        run,
        out_shape=list(outs) + [shape(a.shape, a.dtype) for a in through],
        in_specs=[SMEM] + [HBM if i in hbm else VMEM for i in range(n)] + [HBM] * t,
        out_specs=[VMEM] * o + [HBM] * t,
        scratch_shapes=list(scratch),
        input_output_aliases={1 + n + i: o + i for i in range(t)},
        compiler_params=pltpu.CompilerParams(vmem_limit_bytes=limit * 1024 * 1024),
        cost_estimate=pl.CostEstimate(flops=int(flops), bytes_accessed=int(moved), transcendentals=0),
    )(ids, *arrays, *through)
    return list(results)


def dot(a, b):
    return jnp.dot(a, b, preferred_element_type=F32)


def pool_kernel(slots, ids, seg, enc, out):
    patch = lax.broadcasted_iota(jnp.int32, (slots, seg.shape[1]), 0)
    member = seg[...] == patch
    lengths = jnp.sum(member.astype(F32), axis=1, keepdims=True)
    sums = dot(member.astype(BF16), enc[...])
    pooled = sums / jnp.maximum(lengths, 1.0)
    total = jnp.max(seg[...].astype(F32)) + 1.0
    row = lax.broadcasted_iota(jnp.int32, pooled.shape, 0)
    out[...] = jnp.where(row == slots - 1, total, pooled).astype(BF16)


def pack_kernel(chips, slots, ids, *refs):
    mine, theirs = refs[:chips], refs[chips]
    out, start_out, packed = refs[chips + 1 :]
    q, c = ids[0], ids[1]
    blocks = 2 * chips
    lanes = blocks * slots
    for k in range(chips):
        packed[k * slots : (k + 1) * slots, :] = mine[k][...]
    packed[chips * slots :, :] = theirs[...]
    lane = lax.broadcasted_iota(jnp.int32, (1, lanes), 1)
    block = lane // slots
    patch = lane - block * slots
    part = block // chips
    place = 2 * ((block - part * chips) ^ q) + (part ^ c)
    start = jnp.zeros((1, lanes), F32)
    total = jnp.zeros((1, lanes), F32)
    own = jnp.zeros((1, lanes), F32)
    for b in range(blocks):
        count = packed[(b + 1) * slots - 1 : (b + 1) * slots, 0:lanes].astype(F32)
        where = 2 * ((b % chips) ^ q) + ((b // chips) ^ c)
        start += jnp.where(place > where, count, 0.0)
        total += jnp.where(block == b, count, 0.0)
        own += jnp.where(2 * q + c > where, count, 0.0)
    wanted = (2 * q + c) * ROWS + lax.broadcasted_iota(jnp.int32, (ROWS, lanes), 0)
    found = (start.astype(jnp.int32) + patch == wanted) & (patch < total.astype(jnp.int32))
    out[...] = dot(found.astype(BF16), packed[...]).astype(BF16)
    start_out[...] = jnp.broadcast_to(own[:, 0:HD].astype(jnp.int32), start_out.shape)


def x_kernel(groups, ids, *refs):
    pieces, w, out, packed = refs[:groups], refs[groups], refs[groups + 1], refs[groups + 2]
    for k in range(groups):
        packed[ids[2] ^ k] = pieces[k][...]
    rows = packed[...].reshape(groups * ROWS, packed.shape[2])
    out[...] = dot(rows, w[...]).astype(BF16)


def spread_kernel(groups, chips, ids, *refs):
    pieces, outs, scale, units = refs[:groups], refs[groups : groups + chips], refs[-2], refs[-1]
    q, c, z = ids[0], ids[1], ids[2]
    unit = units.shape[2]
    per = 2 * chips // groups
    for k in range(groups):
        for u in range(per):
            units[(z ^ k) * per + u] = pieces[k][:, u * unit : (u + 1) * unit]
    for k in range(chips):
        for h in range(2):
            outs[k][h] = units[2 * (q ^ k) + (c ^ h)]
    squares = jnp.zeros((units.shape[1], 1), F32)
    for k in range(groups):
        wide = pieces[k][...].astype(F32)
        squares += jnp.sum(wide * wide, axis=1, keepdims=True)
    scale[...] = jnp.broadcast_to(lax.rsqrt(squares / (2 * chips * unit) + norm_epsilon), scale.shape)


def gate_kernel(count, ids, *refs):
    pieces = refs[:count]
    gate_a, gate_b, up_a, up_b = refs[count : count + 4]
    outs = refs[count + 4 :]
    rows, wide = pieces[0].shape[1], gate_a.shape[1]
    a = jnp.concatenate([p[0] for p in pieces], axis=0)
    b = jnp.concatenate([p[1] for p in pieces], axis=0)
    gate = (dot(a, gate_a[...]) + dot(b, gate_b[...])).astype(BF16)
    for k in range(count):
        outs[k][:, :wide] = gate[k * rows : (k + 1) * rows]
    up = (dot(a, up_a[...]) + dot(b, up_b[...])).astype(BF16)
    for k in range(count):
        outs[k][:, wide:] = up[k * rows : (k + 1) * rows]


def hidden_kernel(ids, scale, *refs):
    pieces, out = refs[:-1], refs[-1]
    wide = out.shape[1]
    gate = sum(p[:, :wide].astype(F32) for p in pieces) * scale[:, 0:1]
    up = sum(p[:, wide:].astype(F32) for p in pieces) * scale[:, 0:1]
    out[...] = (gate / (1.0 + jnp.exp(-gate)) * up).astype(BF16)


def down_kernel(count, ids, *refs):
    pieces, w_a, w_b, outs = refs[:count], refs[count], refs[count + 1], refs[count + 2 :]
    rows = pieces[0].shape[0]
    a = jnp.concatenate([p[...] for p in pieces], axis=0)
    for h, w in enumerate((w_a, w_b)):
        y = dot(a, w[...]).astype(BF16)
        for k in range(count):
            outs[k][h] = y[k * rows : (k + 1) * rows]


def regroup_kernel(chips, groups, ids, *refs):
    pieces, outs, units = refs[:chips], refs[chips : chips + groups], refs[chips + groups]
    q, c, z = ids[0], ids[1], ids[2]
    unit = units.shape[2]
    per = 2 * chips // groups
    for k in range(chips):
        for h in range(2):
            units[2 * (q ^ k) + (c ^ h)] = pieces[k][h]
    for k in range(groups):
        for u in range(per):
            outs[k][:, u * unit : (u + 1) * unit] = units[(z ^ k) * per + u]


def out_kernel(groups, ids, *refs):
    pieces, x, w, outs, rows = refs[:groups], refs[groups], refs[groups + 1], refs[groups + 2 : -1], refs[-1]
    down = sum(p[...].astype(F32) for p in pieces)
    residual = (x[...].astype(F32) + down).astype(BF16)
    y = dot(residual, w[...]).astype(BF16)
    rows[...] = y.reshape(rows.shape)
    for k in range(groups):
        outs[k][...] = rows[ids[2] ^ k]


def add_kernel(ids, *refs):
    refs[-1][...] = sum(p[...].astype(F32) for p in refs[:-1]).astype(BF16)


def weights_kernel(ids, seg, dec, keys, out):
    slots = keys.shape[0]
    patch = lax.broadcasted_iota(jnp.int32, (dec.shape[0], slots), 1)
    allowed = patch <= seg[...]
    for h in range(out.shape[0]):
        part = slice(h * HD, (h + 1) * HD)
        scores = lax.dot_general(dec[:, part], keys[:, part], (((1,), (1,)), ((), ())), preferred_element_type=F32)
        scores = jnp.where(allowed, scores / math.sqrt(HD), -1e30)
        expon = jnp.exp(scores - jnp.max(scores, axis=1, keepdims=True))
        out[h] = (expon / jnp.sum(expon, axis=1, keepdims=True)).astype(BF16)


def mix_kernel(chips, ids, *refs):
    mine, theirs = refs[:chips], refs[chips]
    start, weights, dec, out, rows = refs[chips + 1 :]
    q, c = ids[0], ids[1]
    for k in range(chips):
        rows[2 * (q ^ k) + c] = mine[k][...]
        rows[2 * (q ^ k) + 1 - c] = theirs[k]
    every = rows[...].reshape(2 * chips * ROWS, rows.shape[2])
    slots = weights.shape[2]
    patch = lax.broadcasted_iota(jnp.int32, (slots, every.shape[0]), 0)
    position = lax.broadcasted_iota(jnp.int32, (slots, every.shape[0]), 1)
    found = (position - start[0:1, 0:1] == patch).astype(BF16)
    values = dot(found, every).astype(BF16)
    for h in range(weights.shape[0]):
        part = slice(h * HD, (h + 1) * HD)
        out[:, part] = (dec[:, part].astype(F32) + dot(weights[h], values[:, part])).astype(BF16)


def body(enc_states, dec_states, segments, patch_keys, w_in, w_gate, w_up, w_down, w_out):
    seq, groups = lax.axis_size("seq"), lax.axis_size("mp")
    chips = seq // 2
    bytes_, width = enc_states.shape
    slots = patch_keys.shape[0] + 1
    heads = width // HD
    rows = groups * ROWS
    wide = w_in.shape[1]
    unit = w_gate.shape[0]
    ffw = w_gate.shape[1]
    index = lax.axis_index("seq")
    ids = jnp.stack([index // 2, index % 2, lax.axis_index("mp")]).astype(jnp.int32)

    def sibling(a):
        return lax.ppermute(a, "seq", [(i, i ^ 1) for i in range(seq)])

    def chip(a, k):
        return lax.ppermute(a, "seq", [(i, i ^ (2 * k)) for i in range(seq)])

    def plane(a, k):
        return lax.ppermute(a, "mp", [(i, i ^ k) for i in range(groups)])

    [pooled] = call(
        functools.partial(pool_kernel, slots),
        [shape((slots, width))],
        ids,
        segments.reshape(1, bytes_),
        enc_states,
    )
    siblings = [sibling(w) for w in (w_gate, w_up)]
    gathered = [pooled] + [chip(pooled, k) for k in range(1, chips)]
    theirs = sibling(jnp.concatenate(gathered, axis=0))
    packed, start, gate_b, up_b = call(
        functools.partial(pack_kernel, chips, slots),
        [shape((ROWS, width)), shape((8, HD), jnp.int32)],
        ids,
        *gathered,
        theirs,
        through=siblings,
        scratch=[pltpu.VMEM((seq * slots, width), BF16)],
    )
    pieces = [packed] + [plane(packed, k) for k in range(1, groups)]
    x, down_b = call(
        functools.partial(x_kernel, groups),
        [shape((rows, wide))],
        ids,
        *pieces,
        w_in,
        through=[sibling(w_down)],
        scratch=[pltpu.VMEM((groups, ROWS, width), BF16)],
        flops=2 * rows * width * wide,
    )
    pieces = [x] + [plane(x, k) for k in range(1, groups)]
    *sent, scale = call(
        functools.partial(spread_kernel, groups, chips),
        [shape((2, rows, unit)) for _ in range(chips)] + [shape((rows, HD), F32)],
        ids,
        *pieces,
        scratch=[pltpu.VMEM((seq, rows, unit), BF16)],
    )

    def gate(pieces, through=()):
        return call(
            functools.partial(gate_kernel, len(pieces)),
            [shape((rows, 2 * ffw)) for _ in pieces],
            ids,
            *pieces,
            w_gate,
            gate_b,
            w_up,
            up_b,
            through=through,
            flops=8 * len(pieces) * rows * unit * ffw,
        )

    arrived = [chip(sent[k], k) for k in range(1, chips)]
    partial = gate(arrived[:-1])
    last, own = gate(arrived[-1:], [sent[0]])
    partial = [chip(p, k + 1) for k, p in enumerate(partial + [last])]
    partial = gate([own]) + partial

    keys = jnp.pad(patch_keys, ((0, 1), (0, 0)))
    [weights] = call(
        weights_kernel, [shape((heads, bytes_, slots))], ids, segments.reshape(bytes_, 1), dec_states, keys
    )
    hidden, weights = call(hidden_kernel, [shape((rows, ffw))], ids, scale, *partial, through=[weights])

    def down(pieces):
        return call(
            functools.partial(down_kernel, len(pieces)),
            [shape((2, rows, unit)) for _ in pieces],
            ids,
            *pieces,
            w_down,
            down_b,
            flops=4 * len(pieces) * rows * unit * ffw,
        )

    arrived = [chip(hidden, k) for k in range(1, chips)]
    columns = down([hidden]) + down(arrived)
    columns = [columns[0]] + [chip(columns[k], k) for k in range(1, chips)]
    slices = call(
        functools.partial(regroup_kernel, chips, groups),
        [shape((rows, wide)) for _ in range(groups)],
        ids,
        *columns,
        scratch=[pltpu.VMEM((seq, rows, unit), BF16)],
    )
    slices = [slices[0]] + [plane(slices[k], k) for k in range(1, groups)]
    outs = call(
        functools.partial(out_kernel, groups),
        [shape((ROWS, width)) for _ in range(groups)],
        ids,
        *slices,
        x,
        w_out,
        scratch=[pltpu.VMEM((groups, ROWS, width), BF16)],
        flops=2 * rows * width * wide,
    )
    outs = [outs[0]] + [plane(outs[k], k) for k in range(1, groups)]
    [outputs] = call(add_kernel, [shape((ROWS, width))], ids, *outs)
    outputs = [outputs] + [chip(outputs, k) for k in range(1, chips)]
    theirs = sibling(jnp.stack(outputs))
    [decoded] = call(
        functools.partial(mix_kernel, chips),
        [shape((bytes_, width))],
        ids,
        *outputs,
        theirs,
        start,
        weights,
        dec_states,
        scratch=[pltpu.VMEM((seq, ROWS, width), BF16)],
    )
    return decoded


def solution(mesh):
    placed = (
        P(("seq", "mp"), None),
        P(("seq", "mp"), None),
        P(("seq", "mp")),
        P(("seq", "mp"), None),
        P(None, "mp"),
        P("seq", "mp"),
        P("seq", "mp"),
        P("mp", "seq"),
        P("mp", None),
    )
    return jax.shard_map(
        body, mesh=mesh, in_specs=placed, out_specs=P(("seq", "mp"), None), check_vma=False
    )
```

```python
import functools
import math

import jax
import jax.numpy as jnp
from jax import lax
from jax.experimental import pallas as pl
from jax.experimental.pallas import tpu as pltpu
from jax.sharding import PartitionSpec as P

HD = 128
ROWS = 16
norm_epsilon = 1e-05

VMEM = pl.BlockSpec(memory_space=pltpu.VMEM)
SMEM = pl.BlockSpec(memory_space=pltpu.SMEM)
HBM = pl.BlockSpec(memory_space=pl.ANY)
BF16 = jnp.bfloat16
F32 = jnp.float32


def shape(dims, dtype=BF16):
    return jax.ShapeDtypeStruct(tuple(dims), dtype)


def call(kernel, outs, ids, *arrays, after=(), scratch=(), flops=0, limit=20):
    n, t = len(arrays), len(after)

    def run(ids, *refs):
        kernel(ids, *refs[:n], *refs[n + t :])

    moved = sum(a.size * a.dtype.itemsize for a in arrays)
    moved += sum(math.prod(a.shape) * a.dtype.itemsize for a in outs)
    results = pl.pallas_call(
        run,
        out_shape=list(outs),
        in_specs=[SMEM] + [VMEM] * n + [HBM] * t,
        out_specs=[VMEM] * len(outs),
        scratch_shapes=list(scratch),
        compiler_params=pltpu.CompilerParams(vmem_limit_bytes=limit * 1024 * 1024),
        cost_estimate=pl.CostEstimate(flops=int(flops), bytes_accessed=int(moved), transcendentals=0),
    )(ids, *arrays, *after)
    return list(results)


def dot(a, b):
    return jnp.dot(a, b, preferred_element_type=F32)


def pool_kernel(slots, ids, seg, enc, out):
    patch = lax.broadcasted_iota(jnp.int32, (slots, seg.shape[1]), 0)
    member = seg[...] == patch
    lengths = jnp.sum(member.astype(F32), axis=1, keepdims=True)
    sums = dot(member.astype(BF16), enc[...])
    pooled = sums / jnp.maximum(lengths, 1.0)
    total = jnp.max(seg[...].astype(F32)) + 1.0
    row = lax.broadcasted_iota(jnp.int32, pooled.shape, 0)
    out[...] = jnp.where(row == slots - 1, total, pooled).astype(BF16)


def pack_kernel(chips, slots, ids, *refs):
    mine, theirs = refs[:chips], refs[chips]
    out, start_out, packed = refs[chips + 1 :]
    q, c = ids[0], ids[1]
    blocks = 2 * chips
    lanes = blocks * slots
    for k in range(chips):
        packed[k * slots : (k + 1) * slots, :] = mine[k][...]
    packed[chips * slots :, :] = theirs[...]
    lane = lax.broadcasted_iota(jnp.int32, (1, lanes), 1)
    block = lane // slots
    patch = lane - block * slots
    part = block // chips
    place = 2 * ((block - part * chips) ^ q) + (part ^ c)
    start = jnp.zeros((1, lanes), F32)
    total = jnp.zeros((1, lanes), F32)
    own = jnp.zeros((1, lanes), F32)
    for b in range(blocks):
        count = packed[(b + 1) * slots - 1 : (b + 1) * slots, 0:lanes].astype(F32)
        where = 2 * ((b % chips) ^ q) + ((b // chips) ^ c)
        start += jnp.where(place > where, count, 0.0)
        total += jnp.where(block == b, count, 0.0)
        own += jnp.where(2 * q + c > where, count, 0.0)
    wanted = (2 * q + c) * ROWS + lax.broadcasted_iota(jnp.int32, (ROWS, lanes), 0)
    found = (start.astype(jnp.int32) + patch == wanted) & (patch < total.astype(jnp.int32))
    out[...] = dot(found.astype(BF16), packed[...]).astype(BF16)
    start_out[...] = jnp.broadcast_to(own[:, 0:HD].astype(jnp.int32), start_out.shape)


def x_kernel(groups, ids, *refs):
    pieces, w, out, packed = refs[:groups], refs[groups], refs[groups + 1], refs[groups + 2]
    for k in range(groups):
        packed[ids[2] ^ k] = pieces[k][...]
    rows = packed[...].reshape(groups * ROWS, packed.shape[2])
    out[...] = dot(rows, w[...]).astype(BF16)


def spread_kernel(groups, chips, ids, *refs):
    pieces, outs, scale, units = refs[:groups], refs[groups : groups + chips], refs[-2], refs[-1]
    q, c, z = ids[0], ids[1], ids[2]
    unit = units.shape[2]
    per = 2 * chips // groups
    for k in range(groups):
        for u in range(per):
            units[(z ^ k) * per + u] = pieces[k][:, u * unit : (u + 1) * unit]
    for k in range(chips):
        for h in range(2):
            outs[k][h] = units[2 * (q ^ k) + (c ^ h)]
    squares = jnp.zeros((units.shape[1], 1), F32)
    for k in range(groups):
        wide = pieces[k][...].astype(F32)
        squares += jnp.sum(wide * wide, axis=1, keepdims=True)
    scale[...] = jnp.broadcast_to(lax.rsqrt(squares / (2 * chips * unit) + norm_epsilon), scale.shape)


def gate_kernel(count, ids, *refs):
    pieces = refs[:count]
    gate_a, gate_b, up_a, up_b = refs[count : count + 4]
    outs = refs[count + 4 :]
    rows, wide = pieces[0].shape[1], gate_a.shape[1]
    a = jnp.concatenate([p[0] for p in pieces], axis=0)
    b = jnp.concatenate([p[1] for p in pieces], axis=0)
    gate = (dot(a, gate_a[...]) + dot(b, gate_b[...])).astype(BF16)
    for k in range(count):
        outs[k][:, :wide] = gate[k * rows : (k + 1) * rows]
    up = (dot(a, up_a[...]) + dot(b, up_b[...])).astype(BF16)
    for k in range(count):
        outs[k][:, wide:] = up[k * rows : (k + 1) * rows]


def hidden_kernel(ids, scale, *refs):
    pieces, out = refs[:-1], refs[-1]
    wide = out.shape[1]
    gate = sum(p[:, :wide].astype(F32) for p in pieces) * scale[:, 0:1]
    up = sum(p[:, wide:].astype(F32) for p in pieces) * scale[:, 0:1]
    out[...] = (gate / (1.0 + jnp.exp(-gate)) * up).astype(BF16)


def down_kernel(count, ids, *refs):
    pieces, w_a, w_b, outs = refs[:count], refs[count], refs[count + 1], refs[count + 2 :]
    rows = pieces[0].shape[0]
    a = jnp.concatenate([p[...] for p in pieces], axis=0)
    for h, w in enumerate((w_a, w_b)):
        y = dot(a, w[...]).astype(BF16)
        for k in range(count):
            outs[k][h] = y[k * rows : (k + 1) * rows]


def regroup_kernel(chips, groups, ids, *refs):
    pieces, outs, units = refs[:chips], refs[chips : chips + groups], refs[chips + groups]
    q, c, z = ids[0], ids[1], ids[2]
    unit = units.shape[2]
    per = 2 * chips // groups
    for k in range(chips):
        for h in range(2):
            units[2 * (q ^ k) + (c ^ h)] = pieces[k][h]
    for k in range(groups):
        for u in range(per):
            outs[k][:, u * unit : (u + 1) * unit] = units[(z ^ k) * per + u]


def out_kernel(groups, ids, *refs):
    pieces, x, w, outs, rows = refs[:groups], refs[groups], refs[groups + 1], refs[groups + 2 : -1], refs[-1]
    down = sum(p[...].astype(F32) for p in pieces)
    residual = (x[...].astype(F32) + down).astype(BF16)
    y = dot(residual, w[...]).astype(BF16)
    rows[...] = y.reshape(rows.shape)
    for k in range(groups):
        outs[k][...] = rows[ids[2] ^ k]


def add_kernel(ids, *refs):
    refs[-1][...] = sum(p[...].astype(F32) for p in refs[:-1]).astype(BF16)


def weights_kernel(ids, seg, dec, keys, out):
    slots = keys.shape[0]
    patch = lax.broadcasted_iota(jnp.int32, (dec.shape[0], slots), 1)
    allowed = patch <= seg[...]
    for h in range(dec.shape[1] // HD):
        part = slice(h * HD, (h + 1) * HD)
        scores = lax.dot_general(dec[:, part], keys[:, part], (((1,), (1,)), ((), ())), preferred_element_type=F32)
        scores = jnp.where(allowed, scores / math.sqrt(HD), -1e30)
        expon = jnp.exp(scores - jnp.max(scores, axis=1, keepdims=True))
        out[:, h * slots : (h + 1) * slots] = (expon / jnp.sum(expon, axis=1, keepdims=True)).astype(BF16)


def mix_kernel(chips, ids, *refs):
    mine, theirs = refs[:chips], refs[chips]
    start, weights, dec, out, rows = refs[chips + 1 :]
    q, c = ids[0], ids[1]
    for k in range(chips):
        rows[2 * (q ^ k) + c] = mine[k][...]
        rows[2 * (q ^ k) + 1 - c] = theirs[k]
    every = rows[...].reshape(2 * chips * ROWS, rows.shape[2])
    heads = dec.shape[1] // HD
    slots = weights.shape[1] // heads
    patch = lax.broadcasted_iota(jnp.int32, (slots, every.shape[0]), 0)
    position = lax.broadcasted_iota(jnp.int32, (slots, every.shape[0]), 1)
    found = (position - start[0:1, 0:1] == patch).astype(BF16)
    values = dot(found, every).astype(BF16)
    some = max(1, 128 // slots)
    for h in range(0, heads, some):
        n = min(some, heads - h)
        part = slice(h * HD, (h + n) * HD)
        line = lax.broadcasted_iota(jnp.int32, (n * slots, n * HD), 0) // slots
        column = lax.broadcasted_iota(jnp.int32, (n * slots, n * HD), 1) // HD
        spread = jnp.concatenate([values[:, part]] * n, axis=0)
        spread = jnp.where(line == column, spread, jnp.zeros_like(spread))
        mixed = dot(weights[:, h * slots : (h + n) * slots], spread)
        out[:, part] = (dec[:, part].astype(F32) + mixed).astype(BF16)


def body(enc_states, dec_states, segments, patch_keys, w_in, w_gate, w_up, w_down, w_out):
    seq, groups = lax.axis_size("seq"), lax.axis_size("mp")
    chips = seq // 2
    bytes_, width = enc_states.shape
    slots = patch_keys.shape[0] + 1
    heads = width // HD
    rows = groups * ROWS
    wide = w_in.shape[1]
    unit = w_gate.shape[0]
    ffw = w_gate.shape[1]
    index = lax.axis_index("seq")
    ids = jnp.stack([index // 2, index % 2, lax.axis_index("mp")]).astype(jnp.int32)

    def sibling(a):
        return lax.ppermute(a, "seq", [(i, i ^ 1) for i in range(seq)])

    def chip(a, k):
        return lax.ppermute(a, "seq", [(i, i ^ (2 * k)) for i in range(seq)])

    def plane(a, k):
        return lax.ppermute(a, "mp", [(i, i ^ k) for i in range(groups)])

    def chips_of(arrays):
        return [chip(a, k + 1) for k, a in enumerate(arrays)]

    def planes_of(arrays):
        done = [plane(a, k + 1) for k, a in reversed(list(enumerate(arrays)))]
        return done[::-1]

    [pooled] = call(
        functools.partial(pool_kernel, slots),
        [shape((slots, width))],
        ids,
        segments.reshape(1, bytes_),
        enc_states,
    )
    gate_b, up_b = sibling(w_gate), sibling(w_up)
    gathered = [pooled] + chips_of([pooled] * (chips - 1))
    theirs = sibling(jnp.concatenate(gathered, axis=0))
    packed, start = call(
        functools.partial(pack_kernel, chips, slots),
        [shape((ROWS, width)), shape((8, HD), jnp.int32)],
        ids,
        *gathered,
        theirs,
        after=[gate_b, up_b],
        scratch=[pltpu.VMEM((seq * slots, width), BF16)],
    )
    late, packed = lax.optimization_barrier((w_down, packed))
    down_b = sibling(late)
    pieces = [packed] + planes_of([packed] * (groups - 1))
    [x] = call(
        functools.partial(x_kernel, groups),
        [shape((rows, wide))],
        ids,
        *pieces,
        w_in,
        scratch=[pltpu.VMEM((groups, ROWS, width), BF16)],
        flops=2 * rows * width * wide,
    )
    pieces = [x] + planes_of([x] * (groups - 1))
    *sent, scale = call(
        functools.partial(spread_kernel, groups, chips),
        [shape((2, rows, unit)) for _ in range(chips)] + [shape((rows, HD), F32)],
        ids,
        *pieces,
        scratch=[pltpu.VMEM((seq, rows, unit), BF16)],
    )

    def gate(pieces, after=()):
        return call(
            functools.partial(gate_kernel, len(pieces)),
            [shape((rows, 2 * ffw)) for _ in pieces],
            ids,
            *pieces,
            w_gate,
            gate_b,
            w_up,
            up_b,
            after=after,
            flops=8 * len(pieces) * rows * unit * ffw,
        )

    arrived = chips_of(sent[1:])
    partial = gate(arrived[:-1])
    last, own = gate([arrived[-1], sent[0]], partial[:1])
    partial = [own] + chips_of(partial + [last])

    keys = jnp.pad(patch_keys, ((0, 1), (0, 0)))
    [weights] = call(
        weights_kernel, [shape((bytes_, heads * slots))], ids, segments.reshape(bytes_, 1), dec_states, keys
    )
    [hidden] = call(hidden_kernel, [shape((rows, ffw))], ids, scale, *partial, after=[weights])

    def down(pieces):
        return call(
            functools.partial(down_kernel, len(pieces)),
            [shape((2, rows, unit)) for _ in pieces],
            ids,
            *pieces,
            w_down,
            down_b,
            flops=4 * len(pieces) * rows * unit * ffw,
        )

    arrived = chips_of([hidden] * (chips - 1))
    columns = down([hidden]) + down(arrived)
    columns = [columns[0]] + chips_of(columns[1:])
    slices = call(
        functools.partial(regroup_kernel, chips, groups),
        [shape((rows, wide)) for _ in range(groups)],
        ids,
        *columns,
        scratch=[pltpu.VMEM((seq, rows, unit), BF16)],
    )
    slices = [slices[0]] + planes_of(slices[1:])
    outs = call(
        functools.partial(out_kernel, groups),
        [shape((ROWS, width)) for _ in range(groups)],
        ids,
        *slices,
        x,
        w_out,
        scratch=[pltpu.VMEM((groups, ROWS, width), BF16)],
        flops=2 * rows * width * wide,
    )
    outs = [outs[0]] + planes_of(outs[1:])
    [outputs] = call(add_kernel, [shape((ROWS, width))], ids, *outs)
    outputs = [outputs] + chips_of([outputs] * (chips - 1))
    theirs = sibling(jnp.stack(outputs))
    [decoded] = call(
        functools.partial(mix_kernel, chips),
        [shape((bytes_, width))],
        ids,
        *outputs,
        theirs,
        start,
        weights,
        dec_states,
        scratch=[pltpu.VMEM((seq, ROWS, width), BF16)],
    )
    return decoded


def solution(mesh):
    placed = (
        P(("seq", "mp"), None),
        P(("seq", "mp"), None),
        P(("seq", "mp")),
        P(("seq", "mp"), None),
        P(None, "mp"),
        P("seq", "mp"),
        P("seq", "mp"),
        P("mp", "seq"),
        P("mp", None),
    )
    return jax.shard_map(
        body, mesh=mesh, in_specs=placed, out_specs=P(("seq", "mp"), None), check_vma=False
    )
```

```python
import functools
import math

import jax
import jax.numpy as jnp
from jax import lax
from jax.experimental import pallas as pl
from jax.experimental.pallas import tpu as pltpu
from jax.sharding import PartitionSpec as P

HD = 128
ROWS = 16
norm_epsilon = 1e-05

VMEM = pl.BlockSpec(memory_space=pltpu.VMEM)
SMEM = pl.BlockSpec(memory_space=pltpu.SMEM)
HBM = pl.BlockSpec(memory_space=pl.ANY)
BF16 = jnp.bfloat16
F32 = jnp.float32


def shape(dims, dtype=BF16):
    return jax.ShapeDtypeStruct(tuple(dims), dtype)


def call(kernel, outs, ids, *arrays, after=(), scratch=(), flops=0, limit=20):
    n, t = len(arrays), len(after)

    def run(ids, *refs):
        kernel(ids, *refs[:n], *refs[n + t :])

    moved = sum(a.size * a.dtype.itemsize for a in arrays)
    moved += sum(math.prod(a.shape) * a.dtype.itemsize for a in outs)
    results = pl.pallas_call(
        run,
        out_shape=list(outs),
        in_specs=[SMEM] + [VMEM] * n + [HBM] * t,
        out_specs=[VMEM] * len(outs),
        scratch_shapes=list(scratch),
        compiler_params=pltpu.CompilerParams(vmem_limit_bytes=limit * 1024 * 1024),
        cost_estimate=pl.CostEstimate(flops=int(flops), bytes_accessed=int(moved), transcendentals=0),
    )(ids, *arrays, *after)
    return list(results)


def dot(a, b):
    return jnp.dot(a, b, preferred_element_type=F32)


def pool_kernel(slots, ids, seg, enc, out):
    patch = lax.broadcasted_iota(jnp.int32, (slots, seg.shape[1]), 0)
    member = seg[...] == patch
    lengths = jnp.sum(member.astype(F32), axis=1, keepdims=True)
    sums = dot(member.astype(BF16), enc[...])
    pooled = sums / jnp.maximum(lengths, 1.0)
    total = jnp.max(seg[...].astype(F32)) + 1.0
    row = lax.broadcasted_iota(jnp.int32, pooled.shape, 0)
    out[...] = jnp.where(row == slots - 1, total, pooled).astype(BF16)


def pack_kernel(chips, slots, ids, *refs):
    mine, theirs = refs[:chips], refs[chips]
    out, start_out, packed = refs[chips + 1 :]
    q, c = ids[0], ids[1]
    blocks = 2 * chips
    lanes = blocks * slots
    for k in range(chips):
        packed[k * slots : (k + 1) * slots, :] = mine[k][...]
    packed[chips * slots :, :] = theirs[...]
    lane = lax.broadcasted_iota(jnp.int32, (1, lanes), 1)
    block = lane // slots
    patch = lane - block * slots
    part = block // chips
    place = 2 * ((block - part * chips) ^ q) + (part ^ c)
    start = jnp.zeros((1, lanes), F32)
    total = jnp.zeros((1, lanes), F32)
    own = jnp.zeros((1, lanes), F32)
    for b in range(blocks):
        count = packed[(b + 1) * slots - 1 : (b + 1) * slots, 0:lanes].astype(F32)
        where = 2 * ((b % chips) ^ q) + ((b // chips) ^ c)
        start += jnp.where(place > where, count, 0.0)
        total += jnp.where(block == b, count, 0.0)
        own += jnp.where(2 * q + c > where, count, 0.0)
    wanted = (2 * q + c) * ROWS + lax.broadcasted_iota(jnp.int32, (ROWS, lanes), 0)
    found = (start.astype(jnp.int32) + patch == wanted) & (patch < total.astype(jnp.int32))
    out[...] = dot(found.astype(BF16), packed[...]).astype(BF16)
    start_out[...] = jnp.broadcast_to(own[:, 0:HD].astype(jnp.int32), start_out.shape)


def away(k, core, groups):
    return jnp.where(core == 1, 3 - k, k) if k in (1, 2) and groups > 2 else k


def x_kernel(groups, ids, *refs):
    pieces, w, out, packed = refs[:groups], refs[groups], refs[groups + 1], refs[groups + 2]
    for k in range(groups):
        packed[ids[2] ^ k] = pieces[k][...]
    rows = packed[...].reshape(groups * ROWS, packed.shape[2])
    out[...] = dot(rows, w[...]).astype(BF16)


def spread_kernel(groups, chips, ids, *refs):
    pieces, outs, scale, units = refs[:groups], refs[groups : groups + chips], refs[-2], refs[-1]
    q, c, z = ids[0], ids[1], ids[2]
    unit = units.shape[2]
    per = 2 * chips // groups
    for k in range(groups):
        for u in range(per):
            units[(z ^ away(k, c, groups)) * per + u] = pieces[k][:, u * unit : (u + 1) * unit]
    for k in range(chips):
        for h in range(2):
            outs[k][h] = units[2 * (q ^ k) + (c ^ h)]
    squares = jnp.zeros((units.shape[1], 1), F32)
    for k in range(groups):
        wide = pieces[k][...].astype(F32)
        squares += jnp.sum(wide * wide, axis=1, keepdims=True)
    scale[...] = jnp.broadcast_to(lax.rsqrt(squares / (2 * chips * unit) + norm_epsilon), scale.shape)


def gate_kernel(count, ids, *refs):
    pieces = refs[:count]
    gate_a, gate_b, up_a, up_b = refs[count : count + 4]
    outs = refs[count + 4 :]
    rows, wide = pieces[0].shape[1], gate_a.shape[1]
    a = jnp.concatenate([p[0] for p in pieces], axis=0)
    b = jnp.concatenate([p[1] for p in pieces], axis=0)
    gate = (dot(a, gate_a[...]) + dot(b, gate_b[...])).astype(BF16)
    for k in range(count):
        outs[k][:, :wide] = gate[k * rows : (k + 1) * rows]
    up = (dot(a, up_a[...]) + dot(b, up_b[...])).astype(BF16)
    for k in range(count):
        outs[k][:, wide:] = up[k * rows : (k + 1) * rows]


def hidden_kernel(ids, scale, *refs):
    pieces, out = refs[:-1], refs[-1]
    wide = out.shape[1]
    gate = sum(p[:, :wide].astype(F32) for p in pieces) * scale[:, 0:1]
    up = sum(p[:, wide:].astype(F32) for p in pieces) * scale[:, 0:1]
    out[...] = (gate / (1.0 + jnp.exp(-gate)) * up).astype(BF16)


def down_kernel(count, ids, *refs):
    pieces, w_a, w_b, outs = refs[:count], refs[count], refs[count + 1], refs[count + 2 :]
    rows = pieces[0].shape[0]
    a = jnp.concatenate([p[...] for p in pieces], axis=0)
    for h, w in enumerate((w_a, w_b)):
        y = dot(a, w[...]).astype(BF16)
        for k in range(count):
            outs[k][h] = y[k * rows : (k + 1) * rows]


def regroup_kernel(chips, groups, ids, *refs):
    pieces, outs, units = refs[:chips], refs[chips : chips + groups], refs[chips + groups]
    q, c, z = ids[0], ids[1], ids[2]
    unit = units.shape[2]
    per = 2 * chips // groups
    for k in range(chips):
        for h in range(2):
            units[2 * (q ^ k) + (c ^ h)] = pieces[k][h]
    for k in range(groups):
        for u in range(per):
            outs[k][:, u * unit : (u + 1) * unit] = units[(z ^ k) * per + u]


def out_kernel(groups, ids, *refs):
    pieces, x, w, outs, rows = refs[:groups], refs[groups], refs[groups + 1], refs[groups + 2 : -1], refs[-1]
    down = sum(p[...].astype(F32) for p in pieces)
    residual = (x[...].astype(F32) + down).astype(BF16)
    y = dot(residual, w[...]).astype(BF16)
    rows[...] = y.reshape(rows.shape)
    for k in range(groups):
        outs[k][...] = rows[ids[2] ^ k]


def add_kernel(ids, *refs):
    refs[-1][...] = sum(p[...].astype(F32) for p in refs[:-1]).astype(BF16)


def weights_kernel(ids, seg, dec, keys, out):
    slots = keys.shape[0]
    patch = lax.broadcasted_iota(jnp.int32, (dec.shape[0], slots), 1)
    allowed = patch <= seg[...]
    for h in range(dec.shape[1] // HD):
        part = slice(h * HD, (h + 1) * HD)
        scores = lax.dot_general(dec[:, part], keys[:, part], (((1,), (1,)), ((), ())), preferred_element_type=F32)
        scores = jnp.where(allowed, scores / math.sqrt(HD), -1e30)
        expon = jnp.exp(scores - jnp.max(scores, axis=1, keepdims=True))
        out[:, h * slots : (h + 1) * slots] = (expon / jnp.sum(expon, axis=1, keepdims=True)).astype(BF16)


def mix_kernel(chips, ids, *refs):
    mine, theirs = refs[:chips], refs[chips]
    start, weights, dec, out, rows = refs[chips + 1 :]
    q, c = ids[0], ids[1]
    for k in range(chips):
        rows[2 * (q ^ k) + c] = mine[k][...]
        rows[2 * (q ^ k) + 1 - c] = theirs[k]
    every = rows[...].reshape(2 * chips * ROWS, rows.shape[2])
    heads = dec.shape[1] // HD
    slots = weights.shape[1] // heads
    patch = lax.broadcasted_iota(jnp.int32, (slots, every.shape[0]), 0)
    position = lax.broadcasted_iota(jnp.int32, (slots, every.shape[0]), 1)
    found = (position - start[0:1, 0:1] == patch).astype(BF16)
    values = dot(found, every).astype(BF16)
    some = max(1, 128 // slots)
    for h in range(0, heads, some):
        n = min(some, heads - h)
        part = slice(h * HD, (h + n) * HD)
        line = lax.broadcasted_iota(jnp.int32, (n * slots, n * HD), 0) // slots
        column = lax.broadcasted_iota(jnp.int32, (n * slots, n * HD), 1) // HD
        spread = jnp.concatenate([values[:, part]] * n, axis=0)
        spread = jnp.where(line == column, spread, jnp.zeros_like(spread))
        mixed = dot(weights[:, h * slots : (h + n) * slots], spread)
        out[:, part] = (dec[:, part].astype(F32) + mixed).astype(BF16)


def body(enc_states, dec_states, segments, patch_keys, w_in, w_gate, w_up, w_down, w_out):
    seq, groups = lax.axis_size("seq"), lax.axis_size("mp")
    chips = seq // 2
    bytes_, width = enc_states.shape
    slots = patch_keys.shape[0] + 1
    heads = width // HD
    rows = groups * ROWS
    wide = w_in.shape[1]
    unit = w_gate.shape[0]
    ffw = w_gate.shape[1]
    index = lax.axis_index("seq")
    ids = jnp.stack([index // 2, index % 2, lax.axis_index("mp")]).astype(jnp.int32)

    def sibling(a):
        return lax.ppermute(a, "seq", [(i, i ^ 1) for i in range(seq)])

    def chip(a, k):
        return lax.ppermute(a, "seq", [(i, i ^ (2 * k)) for i in range(seq)])

    def plane(a, k):
        return lax.ppermute(a, "mp", [(i, i ^ k) for i in range(groups)])

    def chips_of(arrays):
        return [chip(a, k + 1) for k, a in enumerate(arrays)]

    def plane_by_core(a, k):
        other = 3 - k if k in (1, 2) and groups > 2 else k
        pairs = [(i * groups + z, i * groups + (z ^ (other if i % 2 else k))) for i in range(seq) for z in range(groups)]
        return lax.ppermute(a, ("seq", "mp"), pairs)

    def planes_of(arrays, move=plane):
        done = [move(a, k + 1) for k, a in reversed(list(enumerate(arrays)))]
        return done[::-1]

    [pooled] = call(
        functools.partial(pool_kernel, slots),
        [shape((slots, width))],
        ids,
        segments.reshape(1, bytes_),
        enc_states,
    )
    gate_b, up_b = sibling(w_gate), sibling(w_up)
    gathered = [pooled] + chips_of([pooled] * (chips - 1))
    theirs = sibling(jnp.concatenate(gathered, axis=0))
    packed, start = call(
        functools.partial(pack_kernel, chips, slots),
        [shape((ROWS, width)), shape((8, HD), jnp.int32)],
        ids,
        *gathered,
        theirs,
        after=[gate_b, up_b],
        scratch=[pltpu.VMEM((seq * slots, width), BF16)],
    )
    late, packed = lax.optimization_barrier((w_down, packed))
    down_b = sibling(late)
    pieces = [packed] + planes_of([packed] * (groups - 1))
    [x] = call(
        functools.partial(x_kernel, groups),
        [shape((rows, wide))],
        ids,
        *pieces,
        w_in,
        scratch=[pltpu.VMEM((groups, ROWS, width), BF16)],
        flops=2 * rows * width * wide,
    )
    pieces = [x] + planes_of([x] * (groups - 1), plane_by_core)
    *sent, scale = call(
        functools.partial(spread_kernel, groups, chips),
        [shape((2, rows, unit)) for _ in range(chips)] + [shape((rows, HD), F32)],
        ids,
        *pieces,
        scratch=[pltpu.VMEM((seq, rows, unit), BF16)],
    )

    def gate(pieces, after=()):
        return call(
            functools.partial(gate_kernel, len(pieces)),
            [shape((rows, 2 * ffw)) for _ in pieces],
            ids,
            *pieces,
            w_gate,
            gate_b,
            w_up,
            up_b,
            after=after,
            flops=8 * len(pieces) * rows * unit * ffw,
        )

    arrived = chips_of(sent[1:])
    partial = gate(arrived[:-1])
    last, own = gate([arrived[-1], sent[0]], partial[:1])
    partial = [own] + chips_of(partial + [last])

    keys = jnp.pad(patch_keys, ((0, 1), (0, 0)))
    [weights] = call(
        weights_kernel, [shape((bytes_, heads * slots))], ids, segments.reshape(bytes_, 1), dec_states, keys
    )
    [hidden] = call(hidden_kernel, [shape((rows, ffw))], ids, scale, *partial, after=[weights])

    def down(pieces):
        return call(
            functools.partial(down_kernel, len(pieces)),
            [shape((2, rows, unit)) for _ in pieces],
            ids,
            *pieces,
            w_down,
            down_b,
            flops=4 * len(pieces) * rows * unit * ffw,
        )

    arrived = chips_of([hidden] * (chips - 1))
    columns = down([hidden]) + down(arrived)
    columns = [columns[0]] + chips_of(columns[1:])
    slices = call(
        functools.partial(regroup_kernel, chips, groups),
        [shape((rows, wide)) for _ in range(groups)],
        ids,
        *columns,
        scratch=[pltpu.VMEM((seq, rows, unit), BF16)],
    )
    slices = [slices[0]] + planes_of(slices[1:])
    outs = call(
        functools.partial(out_kernel, groups),
        [shape((ROWS, width)) for _ in range(groups)],
        ids,
        *slices,
        x,
        w_out,
        scratch=[pltpu.VMEM((groups, ROWS, width), BF16)],
        flops=2 * rows * width * wide,
    )
    outs = [outs[0]] + planes_of(outs[1:])
    [outputs] = call(add_kernel, [shape((ROWS, width))], ids, *outs)
    outputs = [outputs] + chips_of([outputs] * (chips - 1))
    theirs = sibling(jnp.stack(outputs))
    [decoded] = call(
        functools.partial(mix_kernel, chips),
        [shape((bytes_, width))],
        ids,
        *outputs,
        theirs,
        start,
        weights,
        dec_states,
        scratch=[pltpu.VMEM((seq, ROWS, width), BF16)],
    )
    return decoded


def solution(mesh):
    placed = (
        P(("seq", "mp"), None),
        P(("seq", "mp"), None),
        P(("seq", "mp")),
        P(("seq", "mp"), None),
        P(None, "mp"),
        P("seq", "mp"),
        P("seq", "mp"),
        P("mp", "seq"),
        P("mp", None),
    )
    return jax.shard_map(
        body, mesh=mesh, in_specs=placed, out_specs=P(("seq", "mp"), None), check_vma=False
    )
```

```python
import functools
import math

import jax
import jax.numpy as jnp
from jax import lax
from jax.experimental import pallas as pl
from jax.experimental.pallas import tpu as pltpu
from jax.sharding import PartitionSpec as P

HD = 128
ROWS = 16
norm_epsilon = 1e-05

VMEM = pl.BlockSpec(memory_space=pltpu.VMEM)
SMEM = pl.BlockSpec(memory_space=pltpu.SMEM)
HBM = pl.BlockSpec(memory_space=pl.ANY)
BF16 = jnp.bfloat16
F32 = jnp.float32


def shape(dims, dtype=BF16):
    return jax.ShapeDtypeStruct(tuple(dims), dtype)


def call(kernel, outs, ids, *arrays, after=(), scratch=(), flops=0, limit=20):
    n, t = len(arrays), len(after)

    def run(ids, *refs):
        kernel(ids, *refs[:n], *refs[n + t :])

    moved = sum(a.size * a.dtype.itemsize for a in arrays)
    moved += sum(math.prod(a.shape) * a.dtype.itemsize for a in outs)
    results = pl.pallas_call(
        run,
        out_shape=list(outs),
        in_specs=[SMEM] + [VMEM] * n + [HBM] * t,
        out_specs=[VMEM] * len(outs),
        scratch_shapes=list(scratch),
        compiler_params=pltpu.CompilerParams(vmem_limit_bytes=limit * 1024 * 1024),
        cost_estimate=pl.CostEstimate(flops=int(flops), bytes_accessed=int(moved), transcendentals=0),
    )(ids, *arrays, *after)
    return list(results)


def dot(a, b):
    return jnp.dot(a, b, preferred_element_type=F32)


def pool_kernel(slots, ids, seg, enc, out):
    patch = lax.broadcasted_iota(jnp.int32, (slots, seg.shape[1]), 0)
    member = seg[...] == patch
    lengths = jnp.sum(member.astype(F32), axis=1, keepdims=True)
    sums = dot(member.astype(BF16), enc[...])
    pooled = sums / jnp.maximum(lengths, 1.0)
    total = jnp.max(seg[...].astype(F32)) + 1.0
    row = lax.broadcasted_iota(jnp.int32, pooled.shape, 0)
    out[...] = jnp.where(row == slots - 1, total, pooled).astype(BF16)


def across(k, core):
    return jnp.where((core == 1) & ((k == 1) | (k == 2)), 3 - k, k)


def pack_kernel(chips, slots, ids, *refs):
    mine, theirs = refs[:chips], refs[chips]
    out, start_out, packed = refs[chips + 1 :]
    q, c = ids[0], ids[1]
    blocks = 2 * chips
    lanes = blocks * slots
    for k in range(chips):
        packed[k * slots : (k + 1) * slots, :] = mine[k][...]
    packed[chips * slots :, :] = theirs[...]
    lane = lax.broadcasted_iota(jnp.int32, (1, lanes), 1)
    block = lane // slots
    patch = lane - block * slots
    part = block // chips
    place = 2 * (across(block - part * chips, part ^ c) ^ q) + (part ^ c)
    start = jnp.zeros((1, lanes), F32)
    total = jnp.zeros((1, lanes), F32)
    own = jnp.zeros((1, lanes), F32)
    for b in range(blocks):
        count = packed[(b + 1) * slots - 1 : (b + 1) * slots, 0:lanes].astype(F32)
        where = 2 * (across(b % chips, (b // chips) ^ c) ^ q) + ((b // chips) ^ c)
        start += jnp.where(place > where, count, 0.0)
        total += jnp.where(block == b, count, 0.0)
        own += jnp.where(2 * q + c > where, count, 0.0)
    wanted = (2 * q + c) * ROWS + lax.broadcasted_iota(jnp.int32, (ROWS, lanes), 0)
    found = (start.astype(jnp.int32) + patch == wanted) & (patch < total.astype(jnp.int32))
    out[...] = dot(found.astype(BF16), packed[...]).astype(BF16)
    start_out[...] = jnp.broadcast_to(own[:, 0:HD].astype(jnp.int32), start_out.shape)


def away(k, core, groups):
    return jnp.where(core == 1, 3 - k, k) if k in (1, 2) and groups > 2 else k


def x_kernel(groups, ids, *refs):
    pieces, w, out, packed = refs[:groups], refs[groups], refs[groups + 1], refs[groups + 2]
    for k in range(groups):
        packed[ids[2] ^ k] = pieces[k][...]
    rows = packed[...].reshape(groups * ROWS, packed.shape[2])
    out[...] = dot(rows, w[...]).astype(BF16)


def spread_kernel(groups, chips, ids, *refs):
    pieces, outs, scale, units = refs[:groups], refs[groups : groups + chips], refs[-2], refs[-1]
    q, c, z = ids[0], ids[1], ids[2]
    unit = units.shape[2]
    per = 2 * chips // groups
    for k in range(groups):
        for u in range(per):
            units[(z ^ away(k, c, groups)) * per + u] = pieces[k][:, u * unit : (u + 1) * unit]
    for k in range(chips):
        for h in range(2):
            outs[k][h] = units[2 * (q ^ k) + (c ^ h)]
    squares = jnp.zeros((units.shape[1], 1), F32)
    for k in range(groups):
        wide = pieces[k][...].astype(F32)
        squares += jnp.sum(wide * wide, axis=1, keepdims=True)
    scale[...] = jnp.broadcast_to(lax.rsqrt(squares / (2 * chips * unit) + norm_epsilon), scale.shape)


def gate_kernel(count, ids, *refs):
    pieces = refs[:count]
    gate_a, gate_b, up_a, up_b = refs[count : count + 4]
    outs = refs[count + 4 :]
    rows, wide = pieces[0].shape[1], gate_a.shape[1]
    a = jnp.concatenate([p[0] for p in pieces], axis=0)
    b = jnp.concatenate([p[1] for p in pieces], axis=0)
    gate = (dot(a, gate_a[...]) + dot(b, gate_b[...])).astype(BF16)
    for k in range(count):
        outs[k][:, :wide] = gate[k * rows : (k + 1) * rows]
    up = (dot(a, up_a[...]) + dot(b, up_b[...])).astype(BF16)
    for k in range(count):
        outs[k][:, wide:] = up[k * rows : (k + 1) * rows]


def hidden_kernel(ids, scale, *refs):
    pieces, out = refs[:-1], refs[-1]
    wide = out.shape[1]
    gate = sum(p[:, :wide].astype(F32) for p in pieces) * scale[:, 0:1]
    up = sum(p[:, wide:].astype(F32) for p in pieces) * scale[:, 0:1]
    out[...] = (gate / (1.0 + jnp.exp(-gate)) * up).astype(BF16)


def down_kernel(count, ids, *refs):
    pieces, w_a, w_b, outs = refs[:count], refs[count], refs[count + 1], refs[count + 2 :]
    rows = pieces[0].shape[0]
    a = jnp.concatenate([p[...] for p in pieces], axis=0)
    for h, w in enumerate((w_a, w_b)):
        y = dot(a, w[...]).astype(BF16)
        for k in range(count):
            outs[k][h] = y[k * rows : (k + 1) * rows]


def regroup_kernel(chips, groups, ids, *refs):
    pieces, outs, units = refs[:chips], refs[chips : chips + groups], refs[chips + groups]
    q, c, z = ids[0], ids[1], ids[2]
    unit = units.shape[2]
    per = 2 * chips // groups
    for k in range(chips):
        for h in range(2):
            units[2 * (q ^ k) + (c ^ h)] = pieces[k][h]
    for k in range(groups):
        for u in range(per):
            outs[k][:, u * unit : (u + 1) * unit] = units[(z ^ k) * per + u]


def out_kernel(groups, ids, *refs):
    pieces, x, w, outs, rows = refs[:groups], refs[groups], refs[groups + 1], refs[groups + 2 : -1], refs[-1]
    down = sum(p[...].astype(F32) for p in pieces)
    residual = (x[...].astype(F32) + down).astype(BF16)
    y = dot(residual, w[...]).astype(BF16)
    rows[...] = y.reshape(rows.shape)
    for k in range(groups):
        outs[k][...] = rows[ids[2] ^ k]


def add_kernel(ids, *refs):
    refs[-1][...] = sum(p[...].astype(F32) for p in refs[:-1]).astype(BF16)


def weights_kernel(ids, seg, dec, keys, out):
    slots = keys.shape[0]
    patch = lax.broadcasted_iota(jnp.int32, (dec.shape[0], slots), 1)
    allowed = patch <= seg[...]
    for h in range(dec.shape[1] // HD):
        part = slice(h * HD, (h + 1) * HD)
        scores = lax.dot_general(dec[:, part], keys[:, part], (((1,), (1,)), ((), ())), preferred_element_type=F32)
        scores = jnp.where(allowed, scores / math.sqrt(HD), -1e30)
        expon = jnp.exp(scores - jnp.max(scores, axis=1, keepdims=True))
        out[:, h * slots : (h + 1) * slots] = (expon / jnp.sum(expon, axis=1, keepdims=True)).astype(BF16)


def mix_kernel(chips, ids, *refs):
    mine, theirs = refs[:chips], refs[chips]
    start, weights, dec, out, rows = refs[chips + 1 :]
    q, c = ids[0], ids[1]
    for k in range(chips):
        rows[2 * (q ^ across(k, c)) + c] = mine[k][...]
        rows[2 * (q ^ across(k, 1 - c)) + 1 - c] = theirs[k]
    every = rows[...].reshape(2 * chips * ROWS, rows.shape[2])
    heads = dec.shape[1] // HD
    slots = weights.shape[1] // heads
    patch = lax.broadcasted_iota(jnp.int32, (slots, every.shape[0]), 0)
    position = lax.broadcasted_iota(jnp.int32, (slots, every.shape[0]), 1)
    found = (position - start[0:1, 0:1] == patch).astype(BF16)
    values = dot(found, every).astype(BF16)
    some = max(1, 128 // slots)
    for h in range(0, heads, some):
        n = min(some, heads - h)
        part = slice(h * HD, (h + n) * HD)
        line = lax.broadcasted_iota(jnp.int32, (n * slots, n * HD), 0) // slots
        column = lax.broadcasted_iota(jnp.int32, (n * slots, n * HD), 1) // HD
        spread = jnp.concatenate([values[:, part]] * n, axis=0)
        spread = jnp.where(line == column, spread, jnp.zeros_like(spread))
        mixed = dot(weights[:, h * slots : (h + n) * slots], spread)
        out[:, part] = (dec[:, part].astype(F32) + mixed).astype(BF16)


def body(enc_states, dec_states, segments, patch_keys, w_in, w_gate, w_up, w_down, w_out):
    seq, groups = lax.axis_size("seq"), lax.axis_size("mp")
    chips = seq // 2
    bytes_, width = enc_states.shape
    slots = patch_keys.shape[0] + 1
    heads = width // HD
    rows = groups * ROWS
    wide = w_in.shape[1]
    unit = w_gate.shape[0]
    ffw = w_gate.shape[1]
    index = lax.axis_index("seq")
    ids = jnp.stack([index // 2, index % 2, lax.axis_index("mp")]).astype(jnp.int32)

    def sibling(a):
        return lax.ppermute(a, "seq", [(i, i ^ 1) for i in range(seq)])

    def chip(a, k):
        return lax.ppermute(a, "seq", [(i, i ^ (2 * k)) for i in range(seq)])

    def plane(a, k):
        return lax.ppermute(a, "mp", [(i, i ^ k) for i in range(groups)])

    def chip_by_core(a, k):
        other = 3 - k if k in (1, 2) and chips > 2 else k
        return lax.ppermute(a, "seq", [(i, i ^ (2 * (other if i % 2 else k))) for i in range(seq)])

    def chips_of(arrays, move=chip):
        return [move(a, k + 1) for k, a in enumerate(arrays)]

    def plane_by_core(a, k):
        other = 3 - k if k in (1, 2) and groups > 2 else k
        pairs = [(i * groups + z, i * groups + (z ^ (other if i % 2 else k))) for i in range(seq) for z in range(groups)]
        return lax.ppermute(a, ("seq", "mp"), pairs)

    def planes_of(arrays, move=plane):
        done = [move(a, k + 1) for k, a in reversed(list(enumerate(arrays)))]
        return done[::-1]

    [pooled] = call(
        functools.partial(pool_kernel, slots),
        [shape((slots, width))],
        ids,
        segments.reshape(1, bytes_),
        enc_states,
    )
    gate_b, up_b = sibling(w_gate), sibling(w_up)
    gathered = [pooled] + chips_of([pooled] * (chips - 1), chip_by_core)
    theirs = sibling(jnp.concatenate(gathered, axis=0))
    packed, start = call(
        functools.partial(pack_kernel, chips, slots),
        [shape((ROWS, width)), shape((8, HD), jnp.int32)],
        ids,
        *gathered,
        theirs,
        after=[gate_b, up_b],
        scratch=[pltpu.VMEM((seq * slots, width), BF16)],
    )
    late, packed = lax.optimization_barrier((w_down, packed))
    down_b = sibling(late)
    pieces = [packed] + planes_of([packed] * (groups - 1))
    [x] = call(
        functools.partial(x_kernel, groups),
        [shape((rows, wide))],
        ids,
        *pieces,
        w_in,
        scratch=[pltpu.VMEM((groups, ROWS, width), BF16)],
        flops=2 * rows * width * wide,
    )
    pieces = [x] + planes_of([x] * (groups - 1), plane_by_core)
    *sent, scale = call(
        functools.partial(spread_kernel, groups, chips),
        [shape((2, rows, unit)) for _ in range(chips)] + [shape((rows, HD), F32)],
        ids,
        *pieces,
        scratch=[pltpu.VMEM((seq, rows, unit), BF16)],
    )

    def gate(pieces, after=()):
        return call(
            functools.partial(gate_kernel, len(pieces)),
            [shape((rows, 2 * ffw)) for _ in pieces],
            ids,
            *pieces,
            w_gate,
            gate_b,
            w_up,
            up_b,
            after=after,
            flops=8 * len(pieces) * rows * unit * ffw,
        )

    arrived = chips_of(sent[1:])
    partial = gate(arrived[:-1])
    last, own = gate([arrived[-1], sent[0]], partial[:1])
    partial = [own] + chips_of(partial + [last])

    keys = jnp.pad(patch_keys, ((0, 1), (0, 0)))
    [weights] = call(
        weights_kernel, [shape((bytes_, heads * slots))], ids, segments.reshape(bytes_, 1), dec_states, keys
    )
    [hidden] = call(hidden_kernel, [shape((rows, ffw))], ids, scale, *partial, after=[weights])

    def down(pieces):
        return call(
            functools.partial(down_kernel, len(pieces)),
            [shape((2, rows, unit)) for _ in pieces],
            ids,
            *pieces,
            w_down,
            down_b,
            flops=4 * len(pieces) * rows * unit * ffw,
        )

    arrived = chips_of([hidden] * (chips - 1))
    columns = down([hidden]) + down(arrived)
    columns = [columns[0]] + chips_of(columns[1:])
    slices = call(
        functools.partial(regroup_kernel, chips, groups),
        [shape((rows, wide)) for _ in range(groups)],
        ids,
        *columns,
        scratch=[pltpu.VMEM((seq, rows, unit), BF16)],
    )
    slices = [slices[0]] + planes_of(slices[1:])
    outs = call(
        functools.partial(out_kernel, groups),
        [shape((ROWS, width)) for _ in range(groups)],
        ids,
        *slices,
        x,
        w_out,
        scratch=[pltpu.VMEM((groups, ROWS, width), BF16)],
        flops=2 * rows * width * wide,
    )
    outs = [outs[0]] + planes_of(outs[1:])
    [outputs] = call(add_kernel, [shape((ROWS, width))], ids, *outs)
    outputs = [outputs] + chips_of([outputs] * (chips - 1), chip_by_core)
    theirs = sibling(jnp.stack(outputs))
    [decoded] = call(
        functools.partial(mix_kernel, chips),
        [shape((bytes_, width))],
        ids,
        *outputs,
        theirs,
        start,
        weights,
        dec_states,
        scratch=[pltpu.VMEM((seq, ROWS, width), BF16)],
    )
    return decoded


def solution(mesh):
    placed = (
        P(("seq", "mp"), None),
        P(("seq", "mp"), None),
        P(("seq", "mp")),
        P(("seq", "mp"), None),
        P(None, "mp"),
        P("seq", "mp"),
        P("seq", "mp"),
        P("mp", "seq"),
        P("mp", None),
    )
    return jax.shard_map(
        body, mesh=mesh, in_specs=placed, out_specs=P(("seq", "mp"), None), check_vma=False
    )
```

```python
import functools
import math

import jax
import jax.numpy as jnp
from jax import lax
from jax.experimental import pallas as pl
from jax.experimental.pallas import tpu as pltpu
from jax.sharding import PartitionSpec as P

HD = 128
ROWS = 16
norm_epsilon = 1e-05

VMEM = pl.BlockSpec(memory_space=pltpu.VMEM)
SMEM = pl.BlockSpec(memory_space=pltpu.SMEM)
HBM = pl.BlockSpec(memory_space=pl.ANY)
BF16 = jnp.bfloat16
F32 = jnp.float32


def shape(dims, dtype=BF16):
    return jax.ShapeDtypeStruct(tuple(dims), dtype)


def call(kernel, outs, ids, *arrays, after=(), scratch=(), flops=0, limit=20):
    n, t = len(arrays), len(after)

    def run(ids, *refs):
        kernel(ids, *refs[:n], *refs[n + t :])

    moved = sum(a.size * a.dtype.itemsize for a in arrays)
    moved += sum(math.prod(a.shape) * a.dtype.itemsize for a in outs)
    results = pl.pallas_call(
        run,
        out_shape=list(outs),
        in_specs=[SMEM] + [VMEM] * n + [HBM] * t,
        out_specs=[VMEM] * len(outs),
        scratch_shapes=list(scratch),
        compiler_params=pltpu.CompilerParams(vmem_limit_bytes=limit * 1024 * 1024),
        cost_estimate=pl.CostEstimate(flops=int(flops), bytes_accessed=int(moved), transcendentals=0),
    )(ids, *arrays, *after)
    return list(results)


def dot(a, b):
    return jnp.dot(a, b, preferred_element_type=F32)


def pool_kernel(slots, ids, seg, enc, out):
    patch = lax.broadcasted_iota(jnp.int32, (slots, seg.shape[1]), 0)
    member = seg[...] == patch
    lengths = jnp.sum(member.astype(F32), axis=1, keepdims=True)
    sums = dot(member.astype(BF16), enc[...])
    pooled = sums / jnp.maximum(lengths, 1.0)
    total = jnp.max(seg[...].astype(F32)) + 1.0
    row = lax.broadcasted_iota(jnp.int32, pooled.shape, 0)
    out[...] = jnp.where(row == slots - 1, total, pooled).astype(BF16)


def across(k, core):
    return jnp.where((core == 1) & ((k == 1) | (k == 2)), 3 - k, k)


def pack_kernel(chips, slots, ids, *refs):
    mine, theirs = refs[:chips], refs[chips]
    out, start_out, packed = refs[chips + 1 :]
    q, c = ids[0], ids[1]
    blocks = 2 * chips
    lanes = blocks * slots
    for k in range(chips):
        packed[k * slots : (k + 1) * slots, :] = mine[k][...]
    packed[chips * slots :, :] = theirs[...]
    lane = lax.broadcasted_iota(jnp.int32, (1, lanes), 1)
    block = lane // slots
    patch = lane - block * slots
    part = block // chips
    place = 2 * (across(block - part * chips, part ^ c) ^ q) + (part ^ c)
    start = jnp.zeros((1, lanes), F32)
    total = jnp.zeros((1, lanes), F32)
    own = jnp.zeros((1, lanes), F32)
    for b in range(blocks):
        count = packed[(b + 1) * slots - 1 : (b + 1) * slots, 0:lanes].astype(F32)
        where = 2 * (across(b % chips, (b // chips) ^ c) ^ q) + ((b // chips) ^ c)
        start += jnp.where(place > where, count, 0.0)
        total += jnp.where(block == b, count, 0.0)
        own += jnp.where(2 * q + c > where, count, 0.0)
    wanted = (2 * q + c) * ROWS + lax.broadcasted_iota(jnp.int32, (ROWS, lanes), 0)
    found = (start.astype(jnp.int32) + patch == wanted) & (patch < total.astype(jnp.int32))
    out[...] = dot(found.astype(BF16), packed[...]).astype(BF16)
    start_out[...] = jnp.broadcast_to(own[:, 0:HD].astype(jnp.int32), start_out.shape)


def away(k, core, groups):
    return jnp.where(core == 1, 3 - k, k) if k in (1, 2) and groups > 2 else k


def x_kernel(groups, ids, *refs):
    pieces, w, out, packed = refs[:groups], refs[groups], refs[groups + 1], refs[groups + 2]
    for k in range(groups):
        packed[ids[2] ^ k] = pieces[k][...]
    rows = packed[...].reshape(groups * ROWS, packed.shape[2])
    out[...] = dot(rows, w[...]).astype(BF16)


def spread_kernel(groups, chips, ids, *refs):
    pieces, outs, scale, units = refs[:groups], refs[groups : groups + chips], refs[-2], refs[-1]
    q, c, z = ids[0], ids[1], ids[2]
    unit = units.shape[2]
    per = 2 * chips // groups
    for k in range(groups):
        for u in range(per):
            units[(z ^ away(k, c, groups)) * per + u] = pieces[k][:, u * unit : (u + 1) * unit]
    for k in range(chips):
        for h in range(2):
            outs[k][h] = units[2 * (q ^ k) + (c ^ h)]
    squares = jnp.zeros((units.shape[1], 1), F32)
    for k in range(groups):
        wide = pieces[k][...].astype(F32)
        squares += jnp.sum(wide * wide, axis=1, keepdims=True)
    scale[...] = jnp.broadcast_to(lax.rsqrt(squares / (2 * chips * unit) + norm_epsilon), scale.shape)


def gate_kernel(count, ids, *refs):
    pieces = refs[:count]
    gate_a, gate_b, up_a, up_b = refs[count : count + 4]
    outs = refs[count + 4 :]
    rows, wide = pieces[0].shape[1], gate_a.shape[1]
    a = jnp.concatenate([p[0] for p in pieces], axis=0)
    b = jnp.concatenate([p[1] for p in pieces], axis=0)
    gate = (dot(a, gate_a[...]) + dot(b, gate_b[...])).astype(BF16)
    for k in range(count):
        outs[k][:, :wide] = gate[k * rows : (k + 1) * rows]
    up = (dot(a, up_a[...]) + dot(b, up_b[...])).astype(BF16)
    for k in range(count):
        outs[k][:, wide:] = up[k * rows : (k + 1) * rows]


def hidden_kernel(ids, scale, *refs):
    pieces, out = refs[:-1], refs[-1]
    wide = out.shape[1]
    gate = sum(p[:, :wide].astype(F32) for p in pieces) * scale[:, 0:1]
    up = sum(p[:, wide:].astype(F32) for p in pieces) * scale[:, 0:1]
    out[...] = (gate / (1.0 + jnp.exp(-gate)) * up).astype(BF16)


def down_kernel(count, ids, *refs):
    pieces, w_a, w_b, outs = refs[:count], refs[count], refs[count + 1], refs[count + 2 :]
    rows = pieces[0].shape[0]
    a = jnp.concatenate([p[...] for p in pieces], axis=0)
    for h, w in enumerate((w_a, w_b)):
        y = dot(a, w[...]).astype(BF16)
        for k in range(count):
            outs[k][h] = y[k * rows : (k + 1) * rows]


def regroup_kernel(chips, groups, ids, *refs):
    pieces, outs, units = refs[:chips], refs[chips : chips + groups], refs[chips + groups]
    q, c, z = ids[0], ids[1], ids[2]
    unit = units.shape[2]
    per = 2 * chips // groups
    for k in range(chips):
        for h in range(2):
            units[2 * (q ^ k) + (c ^ h)] = pieces[k][h]
    for k in range(groups):
        for u in range(per):
            outs[k][:, u * unit : (u + 1) * unit] = units[(z ^ away(k, c, groups)) * per + u]


def out_kernel(groups, ids, *refs):
    pieces, x, w, outs, rows = refs[:groups], refs[groups], refs[groups + 1], refs[groups + 2 : -1], refs[-1]
    down = sum(p[...].astype(F32) for p in pieces)
    residual = (x[...].astype(F32) + down).astype(BF16)
    y = dot(residual, w[...]).astype(BF16)
    rows[...] = y.reshape(rows.shape)
    for k in range(groups):
        outs[k][...] = rows[ids[2] ^ k]


def add_kernel(ids, *refs):
    refs[-1][...] = sum(p[...].astype(F32) for p in refs[:-1]).astype(BF16)


def weights_kernel(ids, seg, dec, keys, out):
    slots = keys.shape[0]
    patch = lax.broadcasted_iota(jnp.int32, (dec.shape[0], slots), 1)
    allowed = patch <= seg[...]
    for h in range(dec.shape[1] // HD):
        part = slice(h * HD, (h + 1) * HD)
        scores = lax.dot_general(dec[:, part], keys[:, part], (((1,), (1,)), ((), ())), preferred_element_type=F32)
        scores = jnp.where(allowed, scores / math.sqrt(HD), -1e30)
        expon = jnp.exp(scores - jnp.max(scores, axis=1, keepdims=True))
        out[:, h * slots : (h + 1) * slots] = (expon / jnp.sum(expon, axis=1, keepdims=True)).astype(BF16)


def mix_kernel(chips, ids, *refs):
    mine, theirs = refs[:chips], refs[chips]
    start, weights, dec, out, rows = refs[chips + 1 :]
    q, c = ids[0], ids[1]
    for k in range(chips):
        rows[2 * (q ^ across(k, c)) + c] = mine[k][...]
        rows[2 * (q ^ across(k, 1 - c)) + 1 - c] = theirs[k]
    every = rows[...].reshape(2 * chips * ROWS, rows.shape[2])
    heads = dec.shape[1] // HD
    slots = weights.shape[1] // heads
    patch = lax.broadcasted_iota(jnp.int32, (slots, every.shape[0]), 0)
    position = lax.broadcasted_iota(jnp.int32, (slots, every.shape[0]), 1)
    found = (position - start[0:1, 0:1] == patch).astype(BF16)
    values = dot(found, every).astype(BF16)
    some = max(1, 128 // slots)
    for h in range(0, heads, some):
        n = min(some, heads - h)
        part = slice(h * HD, (h + n) * HD)
        line = lax.broadcasted_iota(jnp.int32, (n * slots, n * HD), 0) // slots
        column = lax.broadcasted_iota(jnp.int32, (n * slots, n * HD), 1) // HD
        spread = jnp.concatenate([values[:, part]] * n, axis=0)
        spread = jnp.where(line == column, spread, jnp.zeros_like(spread))
        mixed = dot(weights[:, h * slots : (h + n) * slots], spread)
        out[:, part] = (dec[:, part].astype(F32) + mixed).astype(BF16)


def body(enc_states, dec_states, segments, patch_keys, w_in, w_gate, w_up, w_down, w_out):
    seq, groups = lax.axis_size("seq"), lax.axis_size("mp")
    chips = seq // 2
    bytes_, width = enc_states.shape
    slots = patch_keys.shape[0] + 1
    heads = width // HD
    rows = groups * ROWS
    wide = w_in.shape[1]
    unit = w_gate.shape[0]
    ffw = w_gate.shape[1]
    index = lax.axis_index("seq")
    ids = jnp.stack([index // 2, index % 2, lax.axis_index("mp")]).astype(jnp.int32)

    def sibling(a):
        return lax.ppermute(a, "seq", [(i, i ^ 1) for i in range(seq)])

    def chip(a, k):
        return lax.ppermute(a, "seq", [(i, i ^ (2 * k)) for i in range(seq)])

    def plane(a, k):
        return lax.ppermute(a, "mp", [(i, i ^ k) for i in range(groups)])

    def chip_by_core(a, k):
        other = 3 - k if k in (1, 2) and chips > 2 else k
        return lax.ppermute(a, "seq", [(i, i ^ (2 * (other if i % 2 else k))) for i in range(seq)])

    def chips_of(arrays, move=chip):
        return [move(a, k + 1) for k, a in enumerate(arrays)]

    def plane_by_core(a, k):
        other = 3 - k if k in (1, 2) and groups > 2 else k
        pairs = [(i * groups + z, i * groups + (z ^ (other if i % 2 else k))) for i in range(seq) for z in range(groups)]
        return lax.ppermute(a, ("seq", "mp"), pairs)

    def planes_of(arrays, move=plane):
        done = [move(a, k + 1) for k, a in reversed(list(enumerate(arrays)))]
        return done[::-1]

    [pooled] = call(
        functools.partial(pool_kernel, slots),
        [shape((slots, width))],
        ids,
        segments.reshape(1, bytes_),
        enc_states,
    )
    gate_b, up_b = sibling(w_gate), sibling(w_up)
    gathered = [pooled] + chips_of([pooled] * (chips - 1), chip_by_core)
    theirs = sibling(jnp.concatenate(gathered, axis=0))
    packed, start = call(
        functools.partial(pack_kernel, chips, slots),
        [shape((ROWS, width)), shape((8, HD), jnp.int32)],
        ids,
        *gathered,
        theirs,
        after=[gate_b, up_b],
        scratch=[pltpu.VMEM((seq * slots, width), BF16)],
    )
    late, packed = lax.optimization_barrier((w_down, packed))
    down_b = sibling(late)
    pieces = [packed] + planes_of([packed] * (groups - 1))
    [x] = call(
        functools.partial(x_kernel, groups),
        [shape((rows, wide))],
        ids,
        *pieces,
        w_in,
        scratch=[pltpu.VMEM((groups, ROWS, width), BF16)],
        flops=2 * rows * width * wide,
    )
    pieces = [x] + planes_of([x] * (groups - 1), plane_by_core)
    *sent, scale = call(
        functools.partial(spread_kernel, groups, chips),
        [shape((2, rows, unit)) for _ in range(chips)] + [shape((rows, HD), F32)],
        ids,
        *pieces,
        scratch=[pltpu.VMEM((seq, rows, unit), BF16)],
    )

    def gate(pieces, after=()):
        return call(
            functools.partial(gate_kernel, len(pieces)),
            [shape((rows, 2 * ffw)) for _ in pieces],
            ids,
            *pieces,
            w_gate,
            gate_b,
            w_up,
            up_b,
            after=after,
            flops=8 * len(pieces) * rows * unit * ffw,
        )

    arrived = chips_of(sent[1:])
    partial = gate(arrived[:-1])
    last, own = gate([arrived[-1], sent[0]], partial[:1])
    partial = [own] + chips_of(partial + [last])

    keys = jnp.pad(patch_keys, ((0, 1), (0, 0)))
    [weights] = call(
        weights_kernel, [shape((bytes_, heads * slots))], ids, segments.reshape(bytes_, 1), dec_states, keys
    )
    [hidden] = call(hidden_kernel, [shape((rows, ffw))], ids, scale, *partial, after=[weights])

    def down(pieces):
        return call(
            functools.partial(down_kernel, len(pieces)),
            [shape((2, rows, unit)) for _ in pieces],
            ids,
            *pieces,
            w_down,
            down_b,
            flops=4 * len(pieces) * rows * unit * ffw,
        )

    arrived = chips_of([hidden] * (chips - 1))
    columns = down([hidden]) + down(arrived)
    columns = [columns[0]] + chips_of(columns[1:])
    slices = call(
        functools.partial(regroup_kernel, chips, groups),
        [shape((rows, wide)) for _ in range(groups)],
        ids,
        *columns,
        scratch=[pltpu.VMEM((seq, rows, unit), BF16)],
    )
    slices = [slices[0]] + planes_of(slices[1:], plane_by_core)
    outs = call(
        functools.partial(out_kernel, groups),
        [shape((ROWS, width)) for _ in range(groups)],
        ids,
        *slices,
        x,
        w_out,
        scratch=[pltpu.VMEM((groups, ROWS, width), BF16)],
        flops=2 * rows * width * wide,
    )
    outs = [outs[0]] + planes_of(outs[1:])
    [outputs] = call(add_kernel, [shape((ROWS, width))], ids, *outs)
    outputs = [outputs] + chips_of([outputs] * (chips - 1), chip_by_core)
    theirs = sibling(jnp.stack(outputs))
    [decoded] = call(
        functools.partial(mix_kernel, chips),
        [shape((bytes_, width))],
        ids,
        *outputs,
        theirs,
        start,
        weights,
        dec_states,
        scratch=[pltpu.VMEM((seq, ROWS, width), BF16)],
    )
    return decoded


def solution(mesh):
    placed = (
        P(("seq", "mp"), None),
        P(("seq", "mp"), None),
        P(("seq", "mp")),
        P(("seq", "mp"), None),
        P(None, "mp"),
        P("seq", "mp"),
        P("seq", "mp"),
        P("mp", "seq"),
        P("mp", None),
    )
    return jax.shard_map(
        body, mesh=mesh, in_specs=placed, out_specs=P(("seq", "mp"), None), check_vma=False
    )
```
